32 devices in a mesh: row: 8 (over y, x, core), col: 4 (over z).
Axes of the slice: x: 2, y: 2, z: 4, core: 2. Of those that a mesh axis runs over, the one named last changes fastest.
Arguments:
- ket: float32 [8, 4, 2, 81], P('row', 'col'), may hold values from -6 to 6
- corner_tl: bfloat16 [8, 4, 128, 128], P('row', 'col'), may hold values from -6 to 6
- corner_tr: bfloat16 [8, 4, 128, 128], P('row', 'col'), may hold values from -6 to 6
- corner_bl: bfloat16 [8, 4, 128, 128], P('row', 'col'), may hold values from -6 to 6
- edge_left: bfloat16 [8, 4, 128, 9, 128], P('row', 'col'), may hold values from -6 to 6
- edge_top: bfloat16 [8, 4, 128, 9, 128], P('row', 'col'), may hold values from -6 to 6
- edge_right: bfloat16 [8, 4, 128, 9, 128], P('row', 'col'), may hold values from -6 to 6
- edge_bottom: bfloat16 [8, 4, 128, 9, 128], P('row', 'col'), may hold values from -6 to 6
- row_sketch: bfloat16 [8, 4, 2, 1152, 128], P('row', 'col'), may hold values from -0.1875 to 0.1875
- col_sketch: bfloat16 [8, 4, 2, 1152, 128], P('row', 'col'), may hold values from -0.1875 to 0.1875
Outputs:
- edge_left_new: bfloat16 [8, 4, 128, 9, 128], P('row', 'col')
- corner_bl_new: bfloat16 [8, 4, 128, 128], P('row', 'col')
- edge_top_new: bfloat16 [8, 4, 128, 9, 128], P('row', 'col')
- corner_tl_new: bfloat16 [8, 4, 128, 128], P('row', 'col')
- corner_tr_new: bfloat16 [8, 4, 128, 128], P('row', 'col')
The draws below stay inside these ranges and needn't reach their ends.
All inputs are finite; a program needn't handle non-finite values.
Results may differ from the reference program's by a relative error of at most 0.03.
Values may be sent and summed in bfloat16 or wider, within the bound.
No kernel may reach another device: no remote copies, remote signals or barrier semaphores. Data moves between devices by JAX's collectives and lax.ppermute only.
A program may use at most 64 MiB of HBM per device.

```python
import jax
import jax.numpy as jnp
from jax import lax

D = 3
PHYS = 2
CHI = 128
NS_STEPS = 8
D2 = 9
WIN_ROWS = 8
WIN_COLS = 4


def shard_levels(key, extent, pieces, smallest, largest):
    def one(axis_at, shards_of):
        draws = jax.random.uniform(jax.random.fold_in(jax.random.fold_in(key, 6), axis_at), (shards_of,), jnp.float32, smallest / len(pieces), largest / len(pieces))
        return jnp.repeat(jnp.exp(draws), extent[axis_at] // shards_of).reshape((-1,) + (1,) * (len(extent) - axis_at - 1))

    level = one(*pieces[0])
    for cut in pieces[1:]:
        level = level * one(*cut)
    return level


def bell_draw(own_key, dims, scale, most, shards=(), kind=jnp.bfloat16):
    entries = scale * jax.random.normal(own_key, dims, jnp.float32)
    if shards:
        entries = entries * shard_levels(own_key, dims, shards, -0.22, 0.18)
    return jnp.clip(entries, -most, most).astype(kind)


def setup_inputs(seed: int = 0) -> dict:
    key_list = jax.random.split(jax.random.key(seed), 11)
    ket = bell_draw(key_list[0], (WIN_ROWS, WIN_COLS, PHYS, D * D * D * D), 1.0, 6.0, ((0, 8), (1, 4)), jnp.float32)
    corner_tl = bell_draw(key_list[1], (WIN_ROWS, WIN_COLS, CHI, CHI), 1.0, 6.0, ((0, 8), (1, 4)))
    corner_tr = bell_draw(key_list[2], (WIN_ROWS, WIN_COLS, CHI, CHI), 1.0, 6.0, ((0, 8), (1, 4)))
    corner_bl = bell_draw(key_list[3], (WIN_ROWS, WIN_COLS, CHI, CHI), 1.0, 6.0, ((0, 8), (1, 4)))
    edge_left = bell_draw(key_list[4], (WIN_ROWS, WIN_COLS, CHI, D2, CHI), 1.0, 6.0, ((0, 8), (1, 4)))
    edge_top = bell_draw(key_list[5], (WIN_ROWS, WIN_COLS, CHI, D2, CHI), 1.0, 6.0, ((0, 8), (1, 4)))
    edge_right = bell_draw(key_list[6], (WIN_ROWS, WIN_COLS, CHI, D2, CHI), 1.0, 6.0, ((0, 8), (1, 4)))
    edge_bottom = bell_draw(key_list[7], (WIN_ROWS, WIN_COLS, CHI, D2, CHI), 1.0, 6.0, ((0, 8), (1, 4)))
    row_sketch = bell_draw(key_list[8], (WIN_ROWS, WIN_COLS, 2, CHI * D2, CHI), (CHI * D2) ** -0.5, 0.1875, ((0, 8), (1, 4)))
    col_sketch = bell_draw(key_list[9], (WIN_ROWS, WIN_COLS, 2, CHI * D2, CHI), (CHI * D2) ** -0.5, 0.1875, ((0, 8), (1, 4)))
    return dict(ket=ket, corner_tl=corner_tl, corner_tr=corner_tr, corner_bl=corner_bl, edge_left=edge_left, edge_top=edge_top, edge_right=edge_right, edge_bottom=edge_bottom, row_sketch=row_sketch, col_sketch=col_sketch)


def contract(pattern, former, latter):
    return jnp.einsum(pattern, former.astype(jnp.float32), latter.astype(jnp.float32))

def double_layer(ket_site):
    phys_size = ket_site.shape[0]
    tensor = ket_site.reshape(phys_size, D, D, D, D)
    doubled = jnp.einsum('sulda,svmeb->uvlmdeab', tensor, tensor, precision=lax.Precision.HIGHEST)
    return doubled.reshape(D * D, D * D, D * D, D * D).astype(jnp.bfloat16)

def upper_corner(corner, top_edge, left_edge, double_site):
    top_pair = contract('ab,auc->buc', corner, top_edge).astype(jnp.bfloat16)
    upper_half = contract('buc,blg->culg', top_pair, left_edge).astype(jnp.bfloat16)
    enlarged = contract('culg,uldr->crgd', upper_half, double_site).astype(jnp.bfloat16)
    cut_size = enlarged.shape[0] * enlarged.shape[1]
    return (top_pair, enlarged.reshape(cut_size, cut_size))

def lower_corner(corner, bottom_edge, left_edge, double_site):
    bottom_pair = contract('ge,edz->gdz', corner, bottom_edge).astype(jnp.bfloat16)
    lower_half = contract('gdz,blg->zdbl', bottom_pair, left_edge).astype(jnp.bfloat16)
    enlarged = contract('zdbl,uldr->zrbu', lower_half, double_site).astype(jnp.bfloat16)
    cut_size = enlarged.shape[0] * enlarged.shape[1]
    return (bottom_pair, enlarged.reshape(cut_size, cut_size))

def right_corner(corner, top_edge, right_edge, double_site):
    right_pair = contract('ch,hrt->crt', corner, right_edge).astype(jnp.bfloat16)
    right_half = contract('auc,crt->taur', top_edge, right_pair).astype(jnp.bfloat16)
    enlarged = contract('taur,uldr->tdal', right_half, double_site).astype(jnp.bfloat16)
    cut_size = enlarged.shape[0] * enlarged.shape[1]
    return (right_pair, enlarged.reshape(cut_size, cut_size))

def isometry(cut_terms):
    chi_size = cut_terms.shape[1]
    gram = jnp.dot(cut_terms.T, cut_terms, precision=lax.Precision.HIGHEST)
    scaling = jnp.sum(cut_terms * cut_terms) + 1e-06
    identity = jnp.eye(chi_size, dtype=jnp.float32)
    current = gram / scaling
    inverse = identity
    for iteration in range(NS_STEPS):
        factor = 1.5 * identity - 0.5 * jnp.dot(inverse, current, precision=lax.Precision.HIGHEST)
        current = jnp.dot(current, factor, precision=lax.Precision.HIGHEST)
        inverse = jnp.dot(factor, inverse, precision=lax.Precision.HIGHEST)
    result = jnp.dot(cut_terms, inverse, precision=lax.Precision.HIGHEST) / jnp.sqrt(scaling)
    return result.astype(jnp.bfloat16)

def rescale(tensor):
    return (tensor / jnp.sqrt(jnp.mean(tensor * tensor) + 1e-06)).astype(jnp.bfloat16)

def absorb_left(left_edge, double_site, top_pair, bottom_pair, above_iso, below_iso):
    chi_size = left_edge.shape[0]
    bond_size = left_edge.shape[1]
    upper_map = above_iso.reshape(chi_size, bond_size, chi_size)
    lower_map = below_iso.reshape(chi_size, bond_size, chi_size)
    left_first = contract('buk,blg->kulg', upper_map, left_edge).astype(jnp.bfloat16)
    left_second = contract('kulg,uldr->kgdr', left_first, double_site).astype(jnp.bfloat16)
    new_edge = rescale(contract('kgdr,gdm->krm', left_second, lower_map))
    new_top = rescale(contract('buc,buk->ck', top_pair, upper_map))
    new_bottom = rescale(contract('gdz,gdm->mz', bottom_pair, lower_map))
    return (new_edge, new_top, new_bottom)

def absorb_up(top_edge, double_site, corner, left_edge, right_pair, west_map, east_map):
    chi_size = top_edge.shape[0]
    bond_size = top_edge.shape[1]
    west_iso = west_map.reshape(chi_size, bond_size, chi_size)
    east_iso = east_map.reshape(chi_size, bond_size, chi_size)
    top_first = contract('alk,auc->kluc', west_iso, top_edge).astype(jnp.bfloat16)
    top_second = contract('kluc,uldr->kcdr', top_first, double_site).astype(jnp.bfloat16)
    new_edge = rescale(contract('kcdr,crm->kdm', top_second, east_iso))
    left_pair = contract('ab,blg->alg', corner, left_edge).astype(jnp.bfloat16)
    new_left = rescale(contract('alg,alk->kg', left_pair, west_iso))
    new_right = rescale(contract('crt,crm->mt', right_pair, east_iso))
    return (new_edge, new_left, new_right)

def reference(ket, corner_tl, corner_tr, corner_bl, edge_left, edge_top, edge_right, edge_bottom, row_sketch, col_sketch):
    grid_shape = (ket.shape[0], ket.shape[1])

    def flatten_sites(values_in):
        return values_in.reshape((grid_shape[0] * grid_shape[1],) + values_in.shape[2:])

    def unflatten_sites(values_in):
        return values_in.reshape(grid_shape + values_in.shape[1:])

    def site_map(function, operands):
        flat_operands = tuple((flatten_sites(operand) for operand in operands))
        outputs = lax.map(lambda packed: function(*packed), flat_operands)
        return jax.tree.map(unflatten_sites, outputs)
    doubles = site_map(double_layer, (ket,))

    def left_parts(corner, top_edge, left_edge, bottom_corner, bottom_edge, double_site, sketch):
        top_pair, upper_matrix = upper_corner(corner, top_edge, left_edge, double_site)
        bottom_pair, lower_matrix = lower_corner(bottom_corner, bottom_edge, left_edge, double_site)
        upper_term = contract('pq,pk->qk', upper_matrix, sketch[0])
        lower_term = contract('pq,pk->qk', lower_matrix, sketch[1])
        return (top_pair, bottom_pair, upper_term, lower_term)
    top_pairs, bottom_pairs, upper_terms, lower_terms = site_map(left_parts, (corner_tl, edge_top, edge_left, corner_bl, edge_bottom, doubles, row_sketch))
    row_cut = upper_terms + jnp.roll(lower_terms, -1, axis=0)
    row_iso = site_map(isometry, (row_cut,))
    edges_mid, corners_top, corners_bottom = site_map(absorb_left, (edge_left, doubles, top_pairs, bottom_pairs, jnp.roll(row_iso, 1, axis=0), row_iso))
    edge_left_new = jnp.roll(edges_mid, 1, axis=1)
    corner_tl_mid = jnp.roll(corners_top, 1, axis=1)
    corner_bl_new = jnp.roll(corners_bottom, 1, axis=1)

    def col_parts(corner, top_edge, left_edge, other_corner, right_edge, double_site, sketch):
        unused_pair, left_matrix = upper_corner(corner, top_edge, left_edge, double_site)
        right_pair, right_matrix = right_corner(other_corner, top_edge, right_edge, double_site)
        left_term = contract('pq,qk->pk', left_matrix, sketch[0])
        right_term = contract('pq,pk->qk', right_matrix, sketch[1])
        return (right_pair, left_term, right_term)
    right_pairs, left_terms, right_terms = site_map(col_parts, (corner_tl_mid, edge_top, edge_left_new, corner_tr, edge_right, doubles, col_sketch))
    col_cut = left_terms + jnp.roll(right_terms, -1, axis=1)
    col_iso = site_map(isometry, (col_cut,))
    edges_up, corners_left, corners_right = site_map(absorb_up, (edge_top, doubles, corner_tl_mid, edge_left_new, right_pairs, jnp.roll(col_iso, 1, axis=1), col_iso))
    return (edge_left_new, corner_bl_new, jnp.roll(edges_up, 1, axis=0), jnp.roll(corners_left, 1, axis=0), jnp.roll(corners_right, 1, axis=0))
```

```python
import functools

import jax
import jax.numpy as jnp
import numpy as np
from jax import lax
from jax.experimental import pallas as pl
from jax.experimental.pallas import tpu as pltpu
from jax.sharding import PartitionSpec as P

NS_STEPS = 8
PAD = 16
GROUP = 16
F32 = jnp.float32
BF16 = jnp.bfloat16
HIGHEST = lax.Precision.HIGHEST


def ring(axis, steps):
    count = lax.axis_size(axis)
    return [(source, (source + steps) % count) for source in range(count)]


def mul(former, latter):
    return jnp.dot(former, latter, preferred_element_type=F32)


def mul_first(former, latter):
    return lax.dot_general(former, latter, (((0,), (0,)), ((), ())), preferred_element_type=F32)


def mul_exact(former, latter):
    return jnp.dot(former, latter, precision=HIGHEST, preferred_element_type=F32)


def leg_block(flat, leg, chi):
    return flat[:, leg * chi : (leg + 1) * chi]


def stack_legs(flat, legs, chi):
    return jnp.concatenate([leg_block(flat, leg, chi) for leg in range(legs)], axis=0)


def tall_of_native(native_ref, tmp):
    chi, legs, _ = native_ref.shape
    view = tmp.reshape(chi, PAD, tmp.shape[1])
    view[:, :legs, :] = native_ref[...].astype(F32)
    view[:, legs:, :] = jnp.zeros((chi, PAD - legs, tmp.shape[1]), F32)
    return tmp[...].astype(BF16)


def flat_of_tall(tmp, legs):
    chi = tmp.shape[0] // PAD
    return jnp.concatenate([tmp[pl.ds(leg, chi, stride=PAD), :] for leg in range(legs)], axis=1)


def tall_of_flat(flat, tmp, legs):
    chi = tmp.shape[0] // PAD
    for leg in range(legs):
        tmp[pl.ds(leg, chi, stride=PAD), :] = leg_block(flat, leg, chi)
    for leg in range(legs, PAD):
        tmp[pl.ds(leg, chi, stride=PAD), :] = jnp.zeros((chi, tmp.shape[1]), F32)
    return tmp[...].astype(BF16)


def flat_of_rows(rows_ref, tmp, legs):
    count = rows_ref.shape[0]
    chi = count // legs
    tmp[:count, :] = rows_ref[...].astype(F32)
    return jnp.concatenate(
        [tmp[pl.ds(leg, chi, stride=legs), :].astype(BF16) for leg in range(legs)], axis=1
    )


def through_site(block, matrix, chi, legs):
    count = block.shape[0] // PAD
    columns = jnp.concatenate(
        [
            stack_legs(block[one * PAD : (one + 1) * PAD, :], legs, chi)
            for one in range(count)
        ],
        axis=1,
    )
    passed = mul(matrix, columns).astype(BF16)
    return jnp.concatenate(
        [
            jnp.concatenate(
                [
                    passed[leg * PAD : (leg + 1) * PAD, one * chi : (one + 1) * chi]
                    for leg in range(legs)
                ],
                axis=1,
            )
            for one in range(count)
        ],
        axis=0,
    )


def fold_site(start_ref, flat, matrix, end_ref, acc, legs):
    chi = start_ref.shape[1]
    rows = GROUP * PAD
    acc[...] = jnp.zeros_like(acc)

    def step(index, carry):
        here = pl.ds(pl.multiple_of(index * rows, rows), rows)
        block = mul(start_ref[here, :], flat).astype(BF16)
        passed = through_site(block, matrix, chi, legs)
        acc[...] += mul_first(end_ref[here, :], passed)
        return carry

    lax.fori_loop(0, start_ref.shape[0] // rows, step, 0)


def spread_site(start_ref, flat, matrix, end, out, legs):
    chi = start_ref.shape[1]
    rows = GROUP * PAD

    def step(index, carry):
        here = pl.ds(pl.multiple_of(index * rows, rows), rows)
        block = mul(start_ref[here, :], flat).astype(BF16)
        passed = through_site(block, matrix, chi, legs)
        out[here, :] = mul(passed, end)
        return carry

    lax.fori_loop(0, start_ref.shape[0] // rows, step, 0)


def rescaled(value):
    return value * lax.rsqrt(jnp.mean(value * value) + 1e-06)


def inverse_root(gram):
    chi = gram.shape[0]
    rows = lax.broadcasted_iota(jnp.int32, (chi, chi), 0)
    columns = lax.broadcasted_iota(jnp.int32, (chi, chi), 1)
    identity = jnp.where(rows == columns, 1.0, 0.0).astype(F32)
    scaling = jnp.sum(gram * identity) + 1e-06
    current = gram / scaling
    inverse = None
    for iteration in range(NS_STEPS):
        product = current if inverse is None else mul_exact(inverse, current)
        factor = 1.5 * identity - 0.5 * product
        if iteration < NS_STEPS - 1:
            current = mul_exact(current, factor)
        inverse = factor if inverse is None else mul_exact(factor, inverse)
    return inverse * lax.rsqrt(scaling)


def isometry(flat, legs):
    chi = flat.shape[0]
    tall = stack_legs(flat, legs, chi)
    gram = lax.dot_general(
        tall, tall, (((0,), (0,)), ((), ())), precision=HIGHEST, preferred_element_type=F32
    )
    inverse = inverse_root(gram)
    whole = mul_exact(tall, inverse)
    return jnp.concatenate([whole[leg * chi : (leg + 1) * chi] for leg in range(legs)], axis=1)


def lower_kernel(
    ket_ref, pick_ref, corner_ref, bottom_ref, left_ref, sketch_ref,
    lower_ref, pair_ref, left_tall_ref, forth_ref, back_ref, tmp, tmp2,
):
    chi, legs, _ = left_ref.shape
    forth = 0.0
    back = 0.0
    for phys in range(ket_ref.shape[0]):
        row = ket_ref[pl.ds(phys, 1), :]
        factors = []
        for first, second in ((0, 2), (2, 0)):
            for layer in range(2):
                factors.append(
                    lax.dot_general(
                        pick_ref[first + layer] * row, pick_ref[second + layer],
                        (((1,), (1,)), ((), ())), precision=HIGHEST, preferred_element_type=F32,
                    )
                )
        forth = forth + factors[0] * factors[1]
        back = back + factors[2] * factors[3]
    forth = forth.astype(BF16)
    back = back.astype(BF16)
    forth_ref[...] = forth
    back_ref[...] = back
    left_tall_ref[...] = tall_of_native(left_ref, tmp)
    tall_of_native(bottom_ref, tmp)
    bottom = flat_of_tall(tmp, legs).astype(BF16)
    pair = mul(corner_ref[...], bottom).astype(BF16)
    pair_ref[...] = pair
    sketch = flat_of_rows(sketch_ref, tmp, legs)
    spread_site(left_tall_ref, pair, back, stack_legs(sketch, legs, chi), tmp2, legs)
    lower_ref[...] = flat_of_tall(tmp2, legs).astype(BF16)


def upper_kernel(
    corner_ref, top_ref, left_tall_ref, sketch_ref, forth_ref,
    upper_ref, pair_tall_ref, top_tall_ref, tmp, acc,
):
    chi, legs, _ = top_ref.shape
    top_tall_ref[...] = tall_of_native(top_ref, tmp)
    top = flat_of_tall(tmp, legs).astype(BF16)
    pair = mul_first(corner_ref[...], top)
    pair_tall_ref[...] = tall_of_flat(pair, tmp, legs)
    sketch = flat_of_rows(sketch_ref, tmp, legs)
    fold_site(pair_tall_ref, sketch, forth_ref[...], left_tall_ref, acc, legs)
    upper_ref[...] = acc[...].astype(BF16)


def right_kernel(
    corner_ref, right_edge_ref, top_tall_ref, sketch_ref, forth_ref,
    right_ref, pair_ref, tmp, tmp2,
):
    chi, legs, _ = right_edge_ref.shape
    tall_of_native(right_edge_ref, tmp)
    edge = flat_of_tall(tmp, legs).astype(BF16)
    pair = mul(corner_ref[...], edge).astype(BF16)
    pair_ref[...] = pair
    sketch = flat_of_rows(sketch_ref, tmp, legs)
    spread_site(top_tall_ref, pair, forth_ref[...], stack_legs(sketch, legs, chi), tmp2, legs)
    right_ref[...] = flat_of_tall(tmp2, legs).astype(BF16)


def left_move_kernel(
    upper_ref, lower_next_ref, upper_before_ref, lower_ref,
    left_tall_ref, back_ref, pair_tall_ref, bottom_pair_ref,
    edge_ref, top_ref, bottom_ref, tmp, acc, above_tall,
):
    chi = upper_ref.shape[0]
    legs = upper_ref.shape[1] // chi
    below = isometry(upper_ref[...].astype(F32) + lower_next_ref[...].astype(F32), legs)
    above = isometry(upper_before_ref[...].astype(F32) + lower_ref[...].astype(F32), legs)
    below = below.astype(BF16)
    above_tall[...] = tall_of_flat(above, tmp, legs)
    top_ref[...] = rescaled(mul_first(pair_tall_ref[...], above_tall[...])).astype(BF16)
    bottom = mul_first(
        stack_legs(below, legs, chi), stack_legs(bottom_pair_ref[...], legs, chi)
    )
    bottom_ref[...] = rescaled(bottom).astype(BF16)
    fold_site(left_tall_ref, below, back_ref[...], above_tall, acc, legs)
    edge_ref[...] = rescaled(acc[...]).astype(BF16)


def up_cut_kernel(
    corner_ref, edge_ref, top_tall_ref, back_ref, sketch_ref, right_ref,
    iso_ref, pair_tall_ref, edge_out_ref, tmp, acc,
):
    chi = corner_ref.shape[0]
    legs = edge_ref.shape[1] // chi
    edge = edge_ref[...]
    tall_of_flat(edge.astype(F32), tmp, legs)
    edge_out_ref[...] = tmp.reshape(chi, PAD, chi)[:, :legs, :].astype(BF16)
    pair = mul(corner_ref[...], edge)
    pair_tall_ref[...] = tall_of_flat(pair, tmp, legs)
    sketch = flat_of_rows(sketch_ref, tmp, legs)
    fold_site(pair_tall_ref, sketch, back_ref[...], top_tall_ref, acc, legs)
    iso_ref[...] = isometry(acc[...] + right_ref[...].astype(F32), legs).astype(BF16)


def up_move_kernel(
    west_ref, east_ref, top_tall_ref, forth_ref, pair_tall_ref, right_pair_ref,
    edge_ref, left_ref, right_ref, tmp, acc, west_tall,
):
    chi = west_ref.shape[0]
    legs = west_ref.shape[1] // chi
    east = east_ref[...]
    west_tall[...] = tall_of_flat(west_ref[...].astype(F32), tmp, legs)
    left_ref[...] = rescaled(mul_first(west_tall[...], pair_tall_ref[...])).astype(BF16)
    right = mul_first(stack_legs(east, legs, chi), stack_legs(right_pair_ref[...], legs, chi))
    right_ref[...] = rescaled(right).astype(BF16)
    fold_site(top_tall_ref, east, forth_ref[...], west_tall, acc, legs)
    edge_ref[...] = rescaled(acc[...]).astype(BF16)


def native_kernel(flat_ref, out_ref, tmp):
    chi, legs, _ = out_ref.shape
    for leg in range(legs):
        tmp[pl.ds(leg, chi, stride=PAD), :] = leg_block(flat_ref[...], leg, chi).astype(F32)
    out_ref[...] = tmp.reshape(chi, PAD, chi)[:, :legs, :].astype(BF16)


def site_picks(bond, legs):
    rows = np.arange(legs * PAD)
    first, second = rows // PAD, rows % PAD
    index = np.arange(bond**4)
    up, left = index // bond**3, index // bond**2 % bond
    down, right = index // bond % bond, index % bond
    picks = []
    for one, two in ((down, left), (right, up)):
        for layer in range(2):
            big = first // bond if layer == 0 else first % bond
            small = second // bond if layer == 0 else second % bond
            hit = (big[:, None] == one[None, :]) & (small[:, None] == two[None, :])
            picks.append(hit & (second < legs)[:, None])
    return np.stack(picks).astype(np.float32)


def kernel_call(kernel, outs, scratch, *operands):
    return pl.pallas_call(
        kernel,
        out_shape=[jax.ShapeDtypeStruct(shape, BF16) for shape in outs],
        scratch_shapes=[pltpu.VMEM(shape, kind) for shape, kind in scratch],
        compiler_params=pltpu.CompilerParams(vmem_limit_bytes=48 * 2**20),
    )(*operands)


def local(
    ket, corner_tl, corner_tr, corner_bl, edge_left, edge_top, edge_right, edge_bottom,
    row_sketch, col_sketch,
):
    squeeze = lambda value: value.reshape(value.shape[2:])
    ket, corner_tl, corner_tr, corner_bl = map(squeeze, (ket, corner_tl, corner_tr, corner_bl))
    edge_left, edge_top, edge_right, edge_bottom = map(
        squeeze, (edge_left, edge_top, edge_right, edge_bottom)
    )
    row_sketch, col_sketch = map(squeeze, (row_sketch, col_sketch))
    chi, legs, _ = edge_left.shape
    bond = round(legs**0.5)
    flat = (chi, legs * chi)
    tall = (chi * PAD, chi)
    square = (chi, chi)
    site = (legs * PAD, legs * PAD)
    picks = jnp.asarray(site_picks(bond, legs))

    lower, bottom_pair, left_tall, forth, back = kernel_call(
        lower_kernel, [flat, flat, tall, site, site], [(tall, F32), (tall, F32)],
        ket, picks, corner_bl, edge_bottom, edge_left, row_sketch[1],
    )
    lower_next = lax.ppermute(lower, "row", ring("row", -1))
    upper, top_pair_tall, top_tall = kernel_call(
        upper_kernel, [flat, tall, tall], [(tall, F32), (flat, F32)],
        corner_tl, edge_top, left_tall, row_sketch[0], forth,
    )
    upper_before = lax.ppermute(upper, "row", ring("row", 1))
    right, right_pair = kernel_call(
        right_kernel, [flat, flat], [(tall, F32), (tall, F32)],
        corner_tr, edge_right, top_tall, col_sketch[1], forth,
    )
    right_next = lax.ppermute(right, "col", ring("col", -1))
    edge_mid, top_mid, bottom_mid = kernel_call(
        left_move_kernel, [flat, square, square], [(tall, F32), (flat, F32), (tall, BF16)],
        upper, lower_next, upper_before, lower, left_tall, back, top_pair_tall, bottom_pair,
    )
    corner_tl_mid, edge_new, corner_bl_new = lax.ppermute(
        (top_mid, edge_mid, bottom_mid), "col", ring("col", 1)
    )
    col_iso, left_pair_tall, edge_left_new = kernel_call(
        up_cut_kernel, [flat, tall, edge_left.shape], [(tall, F32), (flat, F32)],
        corner_tl_mid, edge_new, top_tall, back, col_sketch[0], right_next,
    )
    west_iso = lax.ppermute(col_iso, "col", ring("col", 1))
    edge_up, left_up, right_up = kernel_call(
        up_move_kernel, [flat, square, square], [(tall, F32), (flat, F32), (tall, BF16)],
        west_iso, col_iso, top_tall, forth, left_pair_tall, right_pair,
    )
    edge_down, corner_tl_new, corner_tr_new = lax.ppermute(
        (edge_up, left_up, right_up), "row", ring("row", 1)
    )
    (edge_top_new,) = kernel_call(
        native_kernel, [edge_top.shape], [(tall, F32)], edge_down
    )
    outs = (edge_left_new, corner_bl_new, edge_top_new, corner_tl_new, corner_tr_new)
    return tuple(value.reshape((1, 1) + value.shape) for value in outs)


def solution(mesh):
    matrix = P("row", "col", None, None)
    tensor = P("row", "col", None, None, None)
    return jax.shard_map(
        local,
        mesh=mesh,
        in_specs=(matrix,) * 4 + (tensor,) * 6,
        out_specs=(tensor, matrix, tensor, matrix, matrix),
        check_vma=False,
    )
```

```python
import jax
import jax.numpy as jnp
import numpy as np
from jax import lax
from jax.experimental import pallas as pl
from jax.experimental.pallas import tpu as pltpu
from jax.sharding import PartitionSpec as P

NS_STEPS = 8
MAIN = 8
F32 = jnp.float32
BF16 = jnp.bfloat16
HIGHEST = lax.Precision.HIGHEST


def ring(axis, steps):
    count = lax.axis_size(axis)
    return [(source, (source + steps) % count) for source in range(count)]


def padded(count, multiple):
    return -(-count // multiple) * multiple


def mul(former, latter):
    return jnp.dot(former, latter, preferred_element_type=F32)


def mul_first(former, latter):
    return lax.dot_general(former, latter, (((0,), (0,)), ((), ())), preferred_element_type=F32)


def beside(parts):
    return jnp.concatenate(parts, axis=1)


def under(parts):
    return jnp.concatenate(parts, axis=0)


def legs_of_flat(flat, chi):
    return [flat[:, start : start + chi] for start in range(0, flat.shape[1], chi)]


def legs_of_first(ref):
    return [ref[leg] for leg in range(ref.shape[0])]


def legs_of_rows(rows, tmp, legs):
    count = rows.shape[0]
    tmp[:count, :] = rows.astype(F32)
    return [
        tmp[pl.ds(leg, count // legs, stride=legs), :].astype(BF16) for leg in range(legs)
    ]


def main_of_legs(parts, tmp):
    chi = parts[0].shape[0]
    for leg in range(MAIN):
        tmp[pl.ds(leg, chi, stride=MAIN), :] = parts[leg].astype(F32)
    return tmp[: chi * MAIN, :].astype(BF16)


def pass_site(main, tails, flat, matrix, side):
    chi = tails[0].shape[0]
    legs = flat.shape[1] // chi
    size = matrix.shape[0]
    first = legs * MAIN
    used = len(tails) * legs
    rows = padded(used, MAIN)
    for index, tail in enumerate(tails):
        for leg, part in enumerate(legs_of_flat(mul(tail, flat), chi)):
            here = (index * legs + leg) * chi
            side[here : here + chi, :] = part
    side[used * chi : rows * chi, :] = jnp.zeros(((rows - used) * chi, chi), F32)
    block = mul(main, flat)
    fill = [jnp.zeros((size - first - rows, chi), F32)] if size > first + rows else []
    columns = beside(
        [
            under(
                legs_of_flat(block[one * MAIN : (one + 1) * MAIN, :], chi)
                + [side[pl.ds(one, rows, stride=chi), :]]
                + fill
            ).astype(BF16)
            for one in range(chi)
        ]
    )
    passed = mul(matrix, columns)
    out = []
    for one in range(chi):
        here = passed[:, one * chi : (one + 1) * chi]
        out.append(beside([here[leg * MAIN : (leg + 1) * MAIN] for leg in range(legs)]))
        side[pl.ds(one, rows, stride=chi), :] = here[first : first + rows]
    out_tails = [
        beside(
            [
                side[(index * legs + leg) * chi : (index * legs + leg + 1) * chi, :]
                for leg in range(legs)
            ]
        ).astype(BF16)
        for index in range(len(tails))
    ]
    return under(out).astype(BF16), out_tails


def fold(end_main, end_tails, main, tails):
    total = mul_first(end_main, main)
    for end, tail in zip(end_tails, tails):
        total = total + mul_first(end, tail)
    return total


def spread(main, tails, end, tmp):
    chi = tails[0].shape[0]
    tmp[: chi * MAIN, :] = mul(main, end)
    parts = [tmp[pl.ds(leg, chi, stride=MAIN), :] for leg in range(MAIN)]
    return beside(parts + [mul(tail, end) for tail in tails])


def rescaled(value):
    return (value * lax.rsqrt(jnp.mean(value * value) + 1e-06)).astype(BF16)


def split(value):
    high = value.astype(BF16)
    return high, (value - high.astype(F32)).astype(BF16)


def mul_split(former, latter):
    (high, low), (other_high, other_low) = former, latter
    return mul(beside([high, low]), under([other_high, other_high])) + mul(high, other_low)


def inverse_root(gram):
    chi = gram.shape[0]
    rows = lax.broadcasted_iota(jnp.int32, (chi, chi), 0)
    columns = lax.broadcasted_iota(jnp.int32, (chi, chi), 1)
    identity = jnp.where(rows == columns, 1.0, 0.0).astype(F32)
    scaling = jnp.sum(gram * identity) + 1e-06
    current = gram / scaling
    inverse = 1.5 * identity - 0.5 * current
    current = mul_split(split(current), split(inverse))
    for iteration in range(1, NS_STEPS):
        now, inv = split(current), split(inverse)
        factor = split(1.5 * identity - 0.5 * mul_split(inv, now))
        if iteration < NS_STEPS - 1:
            both = mul_split(factor, (beside([now[0], inv[0]]), beside([now[1], inv[1]])))
            current, inverse = both[:, :chi], both[:, chi:]
        else:
            inverse = mul_split(factor, inv)
    return inverse * lax.rsqrt(scaling)


def cut_rows(former_ref, latter_ref):
    chi = former_ref.shape[0]
    cut = (former_ref[...].astype(F32) + latter_ref[...].astype(F32)).astype(BF16)
    return under(legs_of_flat(cut, chi))


def iso_legs(former_ref, latter_ref, inverse_ref):
    chi = former_ref.shape[0]
    both = mul(cut_rows(former_ref, latter_ref), inverse_ref[...])
    iso = (both[:, :chi] + both[:, chi:]).astype(BF16)
    return [iso[start : start + chi] for start in range(0, iso.shape[0], chi)]


def site_matrices(ket_ref, pick_ref):
    forth = 0.0
    back = 0.0
    for phys in range(ket_ref.shape[0]):
        row = ket_ref[pl.ds(phys, 1), :]
        factors = []
        for first, second in ((0, 2), (2, 0)):
            for layer in range(2):
                factors.append(
                    lax.dot_general(
                        pick_ref[first + layer] * row, pick_ref[second + layer],
                        (((1,), (1,)), ((), ())), precision=HIGHEST, preferred_element_type=F32,
                    )
                )
        forth = forth + factors[0] * factors[1]
        back = back + factors[2] * factors[3]
    return forth.astype(BF16), back.astype(BF16)


def right_kernel(
    ket_ref, pick_ref, corner_ref, edge_ref, top_ref, sketch_ref,
    right_ref, pair_ref, forth_ref, back_ref, top_main_ref, tmp, side,
):
    forth_ref[...], back_ref[...] = site_matrices(ket_ref, pick_ref)
    legs = edge_ref.shape[0]
    top = legs_of_first(top_ref)
    top_main_ref[...] = main_of_legs(top, tmp)
    pair = mul(corner_ref[...], beside(legs_of_first(edge_ref))).astype(BF16)
    pair_ref[...] = pair
    sketch = under(legs_of_rows(sketch_ref[1], tmp, legs))
    passed, tails = pass_site(top_main_ref[...], top[MAIN:], pair, forth_ref[...], side)
    right_ref[...] = spread(passed, tails, sketch, tmp).astype(BF16)


def lower_kernel(
    corner_ref, bottom_ref, left_ref, sketch_ref, back_ref,
    lower_ref, pair_ref, left_main_ref, tmp, side,
):
    legs = left_ref.shape[0]
    left = legs_of_first(left_ref)
    left_main_ref[...] = main_of_legs(left, tmp)
    pair = mul(corner_ref[...], beside(legs_of_first(bottom_ref))).astype(BF16)
    pair_ref[...] = pair
    sketch = under(legs_of_rows(sketch_ref[1], tmp, legs))
    passed, tails = pass_site(left_main_ref[...], left[MAIN:], pair, back_ref[...], side)
    lower_ref[...] = spread(passed, tails, sketch, tmp).astype(BF16)


def upper_kernel(
    corner_ref, top_ref, left_main_ref, left_ref, sketch_ref, forth_ref,
    upper_ref, pair_ref, tmp, side,
):
    legs, chi, _ = left_ref.shape
    pair = mul_first(corner_ref[...], beside(legs_of_first(top_ref))).astype(BF16)
    pair_ref[...] = pair
    parts = legs_of_flat(pair, chi)
    sketch = beside(legs_of_rows(sketch_ref[0], tmp, legs))
    main = main_of_legs(parts, tmp)
    passed, tails = pass_site(main, parts[MAIN:], sketch, forth_ref[...], side)
    ends = legs_of_first(left_ref)[MAIN:]
    upper_ref[...] = fold(left_main_ref[...], ends, passed, tails).astype(BF16)


def inverse_kernel(former_ref, latter_ref, inverse_ref):
    cut = cut_rows(former_ref, latter_ref)
    inverse_ref[...] = beside(split(inverse_root(mul_first(cut, cut))))


def pass_kernel(
    former_ref, latter_ref, inverse_ref, main_ref, edge_ref, matrix_ref, pair_ref,
    passed_ref, tails_ref, corner_ref, side,
):
    chi = former_ref.shape[0]
    iso = iso_legs(former_ref, latter_ref, inverse_ref)
    pair = under(legs_of_flat(pair_ref[...], chi))
    corner_ref[...] = rescaled(mul_first(under(iso), pair))
    passed, tails = pass_site(
        main_ref[...], legs_of_first(edge_ref)[MAIN:], beside(iso), matrix_ref[...], side
    )
    passed_ref[...] = passed
    for index, tail in enumerate(tails):
        tails_ref[index] = tail


def move_kernel(
    former_ref, latter_ref, inverse_ref, pair_ref, passed_ref, tails_ref,
    edge_ref, corner_ref, tmp, *, pair_first,
):
    chi = former_ref.shape[0]
    iso = iso_legs(former_ref, latter_ref, inverse_ref)
    pair = under(legs_of_flat(pair_ref[...], chi))
    rows = under(iso)
    corner_ref[...] = rescaled(mul_first(pair, rows) if pair_first else mul_first(rows, pair))
    main = main_of_legs(iso, tmp)
    tails = [tails_ref[index] for index in range(tails_ref.shape[0])]
    edge_ref[...] = rescaled(fold(main, iso[MAIN:], passed_ref[...], tails))


def left_cut_kernel(
    corner_ref, edge_ref, top_main_ref, top_ref, back_ref, sketch_ref,
    term_ref, pair_ref, tmp, side,
):
    legs, chi, _ = top_ref.shape
    pair = mul(corner_ref[...], edge_ref[...]).astype(BF16)
    pair_ref[...] = pair
    parts = legs_of_flat(pair, chi)
    sketch = beside(legs_of_rows(sketch_ref[0], tmp, legs))
    main = main_of_legs(parts, tmp)
    passed, tails = pass_site(main, parts[MAIN:], sketch, back_ref[...], side)
    ends = legs_of_first(top_ref)[MAIN:]
    term_ref[...] = fold(top_main_ref[...], ends, passed, tails).astype(BF16)


def store_kernel(count, *refs):
    sources, outs, sems = refs[:count], refs[count : 2 * count], refs[2 * count]
    copies = []
    for index, (source, out) in enumerate(zip(sources, outs)):
        if len(out.shape) == 2:
            copies.append(pltpu.make_async_copy(source, out, sems.at[index, 0]))
            continue
        chi = source.shape[0]
        for leg in range(out.shape[0]):
            part = source.at[:, leg * chi : (leg + 1) * chi]
            copies.append(pltpu.make_async_copy(part, out.at[leg], sems.at[index, leg]))
    for copy in copies:
        copy.start()
    for copy in copies:
        copy.wait()


def site_picks(bond, legs, size):
    order = [(first, second) for first in range(legs) for second in range(MAIN)]
    order += [(first, second) for second in range(MAIN, legs) for first in range(legs)]
    used = len(order)
    first, second = np.array(order + [(0, 0)] * (size - used)).T
    index = np.arange(bond**4)
    up, left = index // bond**3, index // bond**2 % bond
    down, right = index // bond % bond, index % bond
    picks = []
    for one, two in ((down, left), (right, up)):
        for layer in range(2):
            big = first // bond if layer == 0 else first % bond
            small = second // bond if layer == 0 else second % bond
            hit = (big[:, None] == one[None, :]) & (small[:, None] == two[None, :])
            picks.append(hit & (np.arange(size) < used)[:, None])
    return np.stack(picks).astype(np.float32)


def kernel_call(kernel, micros, outs, scratch, *operands):
    return pl.pallas_call(
        kernel,
        out_shape=[jax.ShapeDtypeStruct(shape, BF16) for shape in outs],
        scratch_shapes=[pltpu.VMEM(shape, F32) for shape in scratch],
        compiler_params=pltpu.CompilerParams(vmem_limit_bytes=40 * 2**20),
        cost_estimate=pl.CostEstimate(
            flops=int(micros * 1e9), bytes_accessed=0, transcendentals=0
        ),
    )(*operands)


def store_call(sources, outs):
    legs = max(shape[0] for shape in outs if len(shape) == 3)
    return pl.pallas_call(
        lambda *refs: store_kernel(len(outs), *refs),
        out_shape=[jax.ShapeDtypeStruct(shape, BF16) for shape in outs],
        in_specs=[pl.BlockSpec(memory_space=pltpu.VMEM)] * len(outs),
        out_specs=[pl.BlockSpec(memory_space=pltpu.HBM)] * len(outs),
        scratch_shapes=[pltpu.SemaphoreType.DMA((len(outs), legs))],
    )(*sources)


def local(
    ket, corner_tl, corner_tr, corner_bl, edge_left, edge_top, edge_right, edge_bottom,
    row_sketch, col_sketch,
):
    squeeze = lambda value: value.reshape(value.shape[2:])
    legs_first = lambda value: jnp.swapaxes(squeeze(value), 0, 1)
    ket, corner_tl, corner_tr, corner_bl = map(squeeze, (ket, corner_tl, corner_tr, corner_bl))
    edge_left, edge_top, edge_right, edge_bottom = map(
        legs_first, (edge_left, edge_top, edge_right, edge_bottom)
    )
    row_sketch, col_sketch = map(squeeze, (row_sketch, col_sketch))
    legs, chi, _ = edge_left.shape
    bond = round(legs**0.5)
    size = padded(legs * legs, 32)
    flat = (chi, legs * chi)
    main = (chi * MAIN, chi)
    square = (chi, chi)
    pair_of = (chi, 2 * chi)
    site = (size, size)
    passed_main = (chi * MAIN, legs * chi)
    passed_tails = (legs - MAIN, chi, legs * chi)
    tmp = (chi * legs, chi)
    side = (padded((legs - MAIN) * legs, MAIN) * chi, chi)
    picks = jnp.asarray(site_picks(bond, legs, size))

    right, right_pair, forth, back, top_main = kernel_call(
        right_kernel, 4, [flat, flat, site, site, main], [tmp, side],
        ket, picks, corner_tr, edge_right, edge_top, col_sketch,
    )
    right_next = lax.ppermute(right, "col", ring("col", -1))
    lower, bottom_pair, left_main = kernel_call(
        lower_kernel, 4, [flat, flat, main], [tmp, side],
        corner_bl, edge_bottom, edge_left, row_sketch, back,
    )
    lower_next = lax.ppermute(lower, "row", ring("row", -1))
    upper, top_pair = kernel_call(
        upper_kernel, 4, [flat, flat], [tmp, side],
        corner_tl, edge_top, left_main, edge_left, row_sketch, forth,
    )
    upper_before = lax.ppermute(upper, "row", ring("row", 1))
    right_next, lower_next = lax.optimization_barrier((right_next, lower_next))
    (inverse,) = kernel_call(inverse_kernel, 4, [pair_of], [], upper, lower_next)
    inverse_before = lax.ppermute(inverse, "row", ring("row", 1))
    passed, tails, bottom_mid = kernel_call(
        pass_kernel, 3, [passed_main, passed_tails, square], [side],
        upper, lower_next, inverse, left_main, edge_left, back, bottom_pair,
    )
    corner_bl_new = lax.ppermute(bottom_mid, "col", ring("col", 1))
    edge_mid, top_mid = kernel_call(
        lambda *refs: move_kernel(*refs, pair_first=True), 1, [flat, square], [tmp],
        upper_before, lower, inverse_before, top_pair, passed, tails,
    )
    corner_tl_mid, edge_new = lax.ppermute((top_mid, edge_mid), "col", ring("col", 1))

    term, left_pair = kernel_call(
        left_cut_kernel, 4, [flat, flat], [tmp, side],
        corner_tl_mid, edge_new, top_main, edge_top, back, col_sketch,
    )
    term_before = lax.ppermute(term, "col", ring("col", 1))
    (inverse,) = kernel_call(inverse_kernel, 4, [pair_of], [], term, right_next)
    inverse_before = lax.ppermute(inverse, "col", ring("col", 1))
    passed, tails, right_up = kernel_call(
        pass_kernel, 3, [passed_main, passed_tails, square], [side],
        term, right_next, inverse, top_main, edge_top, forth, right_pair,
    )
    corner_tr_new = lax.ppermute(right_up, "row", ring("row", 1))
    edge_left_new, corner_bl_new = store_call(
        (edge_new, corner_bl_new), (edge_left.shape, square)
    )
    edge_left_new, corner_bl_new, corner_tr_new, passed = lax.optimization_barrier(
        (edge_left_new, corner_bl_new, corner_tr_new, passed)
    )
    edge_up, left_up = kernel_call(
        lambda *refs: move_kernel(*refs, pair_first=False), 1, [flat, square], [tmp],
        term_before, right, inverse_before, left_pair, passed, tails,
    )
    edge_down, corner_tl_new = lax.ppermute((edge_up, left_up), "row", ring("row", 1))
    edge_top_new, corner_tl_new, corner_tr_new = store_call(
        (edge_down, corner_tl_new, corner_tr_new), (edge_top.shape, square, square)
    )
    outs = (
        jnp.swapaxes(edge_left_new, 0, 1), corner_bl_new,
        jnp.swapaxes(edge_top_new, 0, 1), corner_tl_new, corner_tr_new,
    )
    return tuple(value.reshape((1, 1) + value.shape) for value in outs)


def solution(mesh):
    matrix = P("row", "col", None, None)
    tensor = P("row", "col", None, None, None)
    return jax.shard_map(
        local,
        mesh=mesh,
        in_specs=(matrix,) * 4 + (tensor,) * 6,
        out_specs=(tensor, matrix, tensor, matrix, matrix),
        check_vma=False,
    )
```

```python
import functools

import jax
import jax.numpy as jnp
from jax import lax
from jax.experimental import pallas as pl
from jax.experimental.pallas import tpu as pltpu
from jax.sharding import PartitionSpec as P

NS_STEPS = 8
MAIN = 8
F32 = jnp.float32
BF16 = jnp.bfloat16
HIGHEST = lax.Precision.HIGHEST


def ring(axis, steps):
    count = lax.axis_size(axis)
    return [(source, (source + steps) % count) for source in range(count)]


def diagonal():
    rows, cols = lax.axis_size("row"), lax.axis_size("col")
    return [
        (row * cols + col, (row + 1) % rows * cols + (col + 1) % cols)
        for row in range(rows)
        for col in range(cols)
    ]


def padded(count, multiple):
    return -(-count // multiple) * multiple


def mul(former, latter):
    return jnp.dot(former, latter, preferred_element_type=F32)


def mul_first(former, latter):
    return lax.dot_general(former, latter, (((0,), (0,)), ((), ())), preferred_element_type=F32)


def beside(parts):
    return jnp.concatenate(parts, axis=1)


def under(parts):
    return jnp.concatenate(parts, axis=0)


def legs_of_flat(flat, chi):
    return [flat[:, start : start + chi] for start in range(0, flat.shape[1], chi)]


def legs_of_first(ref):
    return [ref[leg] for leg in range(ref.shape[0])]


def legs_of_rows(rows, tmp, legs):
    count = rows.shape[0]
    tmp[:count, :] = rows.astype(F32)
    return [
        tmp[pl.ds(leg, count // legs, stride=legs), :].astype(BF16) for leg in range(legs)
    ]


def main_of_legs(parts, tmp):
    chi = parts[0].shape[0]
    for leg in range(MAIN):
        tmp[pl.ds(leg, chi, stride=MAIN), :] = parts[leg].astype(F32)
    return tmp[: chi * MAIN, :].astype(BF16)


def pass_site(main, tails, flat, matrix, side):
    chi = tails[0].shape[0]
    legs = flat.shape[1] // chi
    size = matrix.shape[0]
    first = legs * MAIN
    used = len(tails) * legs
    rows = padded(used, MAIN)
    for index, tail in enumerate(tails):
        for leg, part in enumerate(legs_of_flat(mul(tail, flat), chi)):
            here = (index * legs + leg) * chi
            side[here : here + chi, :] = part
    side[used * chi : rows * chi, :] = jnp.zeros(((rows - used) * chi, chi), F32)
    block = mul(main, flat)
    fill = [jnp.zeros((size - first - rows, chi), F32)] if size > first + rows else []
    columns = beside(
        [
            under(
                legs_of_flat(block[one * MAIN : (one + 1) * MAIN, :], chi)
                + [side[pl.ds(one, rows, stride=chi), :]]
                + fill
            ).astype(BF16)
            for one in range(chi)
        ]
    )
    passed = mul(matrix, columns)
    out = []
    for one in range(chi):
        here = passed[:, one * chi : (one + 1) * chi]
        out.append(beside([here[leg * MAIN : (leg + 1) * MAIN] for leg in range(legs)]))
        side[pl.ds(one, rows, stride=chi), :] = here[first : first + rows]
    out_tails = [
        beside(
            [
                side[(index * legs + leg) * chi : (index * legs + leg + 1) * chi, :]
                for leg in range(legs)
            ]
        ).astype(BF16)
        for index in range(len(tails))
    ]
    return under(out).astype(BF16), out_tails


def fold(end_main, end_tails, main, tails):
    total = mul_first(end_main, main)
    for end, tail in zip(end_tails, tails):
        total = total + mul_first(end, tail)
    return total


def spread(main, tails, end, tmp):
    chi = tails[0].shape[0]
    tmp[: chi * MAIN, :] = mul(main, end)
    parts = [tmp[pl.ds(leg, chi, stride=MAIN), :] for leg in range(MAIN)]
    return beside(parts + [mul(tail, end) for tail in tails])


def rescaled(value):
    return (value * lax.rsqrt(jnp.mean(value * value) + 1e-06)).astype(BF16)


def split(value):
    high = value.astype(BF16)
    return high, (value - high.astype(F32)).astype(BF16)


def mul_split(former, latter):
    (high, low), (other_high, other_low) = former, latter
    return mul(beside([high, low]), under([other_high, other_high])) + mul(high, other_low)


def inverse_roots(grams):
    chi = grams[0].shape[0]
    rows = lax.broadcasted_iota(jnp.int32, (chi, chi), 0)
    columns = lax.broadcasted_iota(jnp.int32, (chi, chi), 1)
    identity = jnp.where(rows == columns, 1.0, 0.0).astype(F32)
    scalings = [jnp.sum(gram * identity) + 1e-06 for gram in grams]
    currents = [gram / scaling for gram, scaling in zip(grams, scalings)]
    inverses = [1.5 * identity - 0.5 * current for current in currents]
    currents = [
        mul_split(split(current), split(inverse))
        for current, inverse in zip(currents, inverses)
    ]
    for iteration in range(1, NS_STEPS):
        nows = [split(current) for current in currents]
        invs = [split(inverse) for inverse in inverses]
        factors = [
            split(1.5 * identity - 0.5 * mul_split(inv, now)) for inv, now in zip(invs, nows)
        ]
        if iteration < NS_STEPS - 1:
            boths = [
                mul_split(factor, (beside([now[0], inv[0]]), beside([now[1], inv[1]])))
                for factor, now, inv in zip(factors, nows, invs)
            ]
            currents = [both[:, :chi] for both in boths]
            inverses = [both[:, chi:] for both in boths]
        else:
            inverses = [mul_split(factor, inv) for factor, inv in zip(factors, invs)]
    return [
        beside(split(inverse * lax.rsqrt(scaling)))
        for inverse, scaling in zip(inverses, scalings)
    ]


def site_picks(bond, legs, size):
    shape = (size, bond**4)
    row = lax.broadcasted_iota(jnp.int32, shape, 0)
    column = lax.broadcasted_iota(jnp.int32, shape, 1)
    digit = lambda value, place: lax.rem(lax.div(value, bond**place), bond)
    late = row - legs * MAIN
    first = jnp.where(late < 0, lax.div(row, MAIN), lax.rem(jnp.maximum(late, 0), legs))
    second = jnp.where(
        late < 0, lax.rem(row, MAIN), MAIN + lax.div(jnp.maximum(late, 0), legs)
    )
    up, left, down, right = (digit(column, place) for place in (3, 2, 1, 0))
    picks = []
    for one, two in ((down, left), (right, up)):
        for place in (1, 0):
            hit = (digit(first, place) == one) & (digit(second, place) == two)
            picks.append(jnp.where(hit & (row < legs * legs), 1.0, 0.0).astype(F32))
    return picks


def site_kernel(ket_ref, forth_ref, back_ref, *, bond, legs):
    picks = site_picks(bond, legs, forth_ref.shape[0])
    forth = 0.0
    back = 0.0
    for phys in range(ket_ref.shape[0]):
        row = ket_ref[pl.ds(phys, 1), :]
        factors = []
        for first, second in ((0, 2), (2, 0)):
            for layer in range(2):
                factors.append(
                    lax.dot_general(
                        picks[first + layer] * row, picks[second + layer],
                        (((1,), (1,)), ((), ())), precision=HIGHEST, preferred_element_type=F32,
                    )
                )
        forth = forth + factors[0] * factors[1]
        back = back + factors[2] * factors[3]
    forth_ref[...] = forth.astype(BF16)
    back_ref[...] = back.astype(BF16)


def lower_kernel(
    corner_ref, bottom_ref, left_ref, sketch_ref, back_ref,
    lower_ref, pair_ref, left_main_ref, tmp, side,
):
    legs = left_ref.shape[0]
    left = legs_of_first(left_ref)
    left_main_ref[...] = main_of_legs(left, tmp)
    pair = mul(corner_ref[...], beside(legs_of_first(bottom_ref))).astype(BF16)
    pair_ref[...] = pair
    folded = under(legs_of_rows(sketch_ref[1], tmp, legs))
    passed, tails = pass_site(left_main_ref[...], left[MAIN:], pair, back_ref[...], side)
    lower_ref[...] = spread(passed, tails, folded, tmp).astype(BF16)


def right_kernel(
    corner_ref, edge_ref, top_ref, sketch_ref, forth_ref,
    right_ref, pair_ref, top_main_ref, tmp, side,
):
    legs = edge_ref.shape[0]
    top = legs_of_first(top_ref)
    top_main_ref[...] = main_of_legs(top, tmp)
    pair = mul(corner_ref[...], beside(legs_of_first(edge_ref))).astype(BF16)
    pair_ref[...] = pair
    folded = under(legs_of_rows(sketch_ref[1], tmp, legs))
    passed, tails = pass_site(top_main_ref[...], top[MAIN:], pair, forth_ref[...], side)
    right_ref[...] = spread(passed, tails, folded, tmp).astype(BF16)


def upper_kernel(
    corner_ref, top_ref, left_main_ref, left_ref, sketch_ref, forth_ref,
    upper_ref, pair_ref, tmp, side,
):
    legs, chi, _ = left_ref.shape
    pair = mul_first(corner_ref[...], beside(legs_of_first(top_ref))).astype(BF16)
    pair_ref[...] = pair
    parts = legs_of_flat(pair, chi)
    sketch = beside(legs_of_rows(sketch_ref[0], tmp, legs))
    main = main_of_legs(parts, tmp)
    passed, tails = pass_site(main, parts[MAIN:], sketch, forth_ref[...], side)
    ends = legs_of_first(left_ref)[MAIN:]
    upper_ref[...] = fold(left_main_ref[...], ends, passed, tails).astype(BF16)


def cut_legs(former_ref, latter_ref):
    chi = former_ref.shape[0]
    cut = former_ref[...].astype(F32) + latter_ref[...].astype(F32)
    return legs_of_flat(cut.astype(BF16), chi)


def halves(value):
    chi = value.shape[1] // 2
    return value[:, :chi] + value[:, chi:]


def right_times(value, inverse):
    return halves(mul(value, inverse))


def left_times(inverse, value):
    chi = inverse.shape[0]
    both = mul_first(inverse, value)
    return both[:chi] + both[chi:]


def inverse_kernel(former_ref, latter_ref, pair_ref, inverse_ref, corner_ref):
    cut = under(cut_legs(former_ref, latter_ref))
    pair = under(legs_of_flat(pair_ref[...], former_ref.shape[0]))
    (inverse,) = inverse_roots([mul_first(cut, cut)])
    inverse_ref[...] = inverse
    corner_ref[...] = rescaled(left_times(inverse, mul_first(cut, pair).astype(BF16)))


def pass_kernel(
    former_ref, latter_ref, main_ref, edge_ref, matrix_ref, passed_ref, tails_ref, side
):
    cut = cut_legs(former_ref, latter_ref)
    passed, tails = pass_site(
        main_ref[...], legs_of_first(edge_ref)[MAIN:], beside(cut), matrix_ref[...], side
    )
    passed_ref[...] = passed
    for index, tail in enumerate(tails):
        tails_ref[index] = tail


def folded_cut(cut, passed_ref, tails_ref, tmp):
    tails = [tails_ref[index] for index in range(tails_ref.shape[0])]
    return fold(main_of_legs(cut, tmp), cut[MAIN:], passed_ref[...], tails).astype(BF16)


def left_move_kernel(
    upper_ref, lower_next_ref, upper_before_ref, lower_ref, top_pair_ref, bottom_pair_ref,
    passed_ref, tails_ref, moved_ref, tmp,
):
    chi = upper_ref.shape[0]
    below = cut_legs(upper_ref, lower_next_ref)
    above = cut_legs(upper_before_ref, lower_ref)
    rows_below, rows_above = under(below), under(above)
    top = mul_first(under(legs_of_flat(top_pair_ref[...], chi)), rows_above).astype(BF16)
    bottom = mul_first(rows_below, under(legs_of_flat(bottom_pair_ref[...], chi))).astype(BF16)
    edge = folded_cut(above, passed_ref, tails_ref, tmp)
    inverse_below, inverse_above = inverse_roots(
        [mul_first(rows_below, rows_below), mul_first(rows_above, rows_above)]
    )
    turned = left_times(inverse_above, edge).astype(BF16)
    rows = rescaled(right_times(under(legs_of_flat(turned, chi)), inverse_below))
    moved_ref[...] = beside(
        [rows[start : start + chi] for start in range(0, rows.shape[0], chi)]
        + [
            rescaled(right_times(top, inverse_above)),
            rescaled(left_times(inverse_below, bottom)),
        ]
    )


def left_cut_kernel(
    moved_ref, top_main_ref, top_ref, back_ref, sketch_ref,
    edge_ref, bottom_ref, term_ref, pair_ref, tmp, side, sems,
):
    legs, chi, _ = top_ref.shape
    part = lambda leg: moved_ref.at[:, leg * chi : (leg + 1) * chi]
    outs = [edge_ref.at[leg] for leg in range(legs)]
    stores = [pltpu.make_async_copy(part(leg), outs[leg], sems.at[leg]) for leg in range(legs)]
    stores.append(pltpu.make_async_copy(part(legs + 1), bottom_ref, sems.at[legs]))
    for store in stores:
        store.start()
    corner = moved_ref[:, legs * chi : (legs + 1) * chi]
    pair = mul(corner, moved_ref[:, : legs * chi]).astype(BF16)
    pair_ref[...] = pair
    parts = legs_of_flat(pair, chi)
    sketch = beside(legs_of_rows(sketch_ref[0], tmp, legs))
    main = main_of_legs(parts, tmp)
    passed, tails = pass_site(main, parts[MAIN:], sketch, back_ref[...], side)
    ends = legs_of_first(top_ref)[MAIN:]
    term_ref[...] = fold(top_main_ref[...], ends, passed, tails).astype(BF16)
    for store in stores:
        store.wait()


def up_move_kernel(
    term_before_ref, right_ref, left_pair_ref, passed_ref, tails_ref, inverse_ref, corner_ref,
    moved_ref, tmp,
):
    chi = right_ref.shape[0]
    west = cut_legs(term_before_ref, right_ref)
    left = mul_first(under(west), under(legs_of_flat(left_pair_ref[...], chi)))
    edge = under(legs_of_flat(folded_cut(west, passed_ref, tails_ref, tmp), chi))
    rows = right_times(edge, inverse_ref[...]).astype(BF16)
    moved_ref[...] = beside(
        [rows[start : start + chi] for start in range(0, rows.shape[0], chi)]
        + [left.astype(BF16), corner_ref[...]]
    )


def finish_kernel(
    moved_ref, west_ref, edge_ref, left_ref, right_ref, edge, left, sems
):
    legs, chi, _ = edge.shape
    stores = [
        pltpu.make_async_copy(moved_ref.at[:, (legs + 1) * chi :], right_ref, sems.at[0])
    ]
    stores[0].start()
    both = left_times(west_ref[...], moved_ref[:, : (legs + 1) * chi])
    left[...] = rescaled(both[:, legs * chi :])
    stores.append(pltpu.make_async_copy(left, left_ref, sems.at[1]))
    stores[1].start()
    flat = rescaled(both[:, : legs * chi])
    for leg, part in enumerate(legs_of_flat(flat, chi)):
        edge[leg] = part
    stores.append(pltpu.make_async_copy(edge, edge_ref, sems.at[2]))
    stores[2].start()
    for store in stores:
        store.wait()


def kernel_call(kernel, micros, outs, scratch, *operands, stores=0):
    place = lambda own: pl.BlockSpec(memory_space=pltpu.HBM if own else pltpu.VMEM)
    return pl.pallas_call(
        kernel,
        out_shape=[jax.ShapeDtypeStruct(shape, BF16) for shape in outs],
        in_specs=[place(False)] * len(operands),
        out_specs=[place(index < stores) for index in range(len(outs))],
        scratch_shapes=scratch,
        compiler_params=pltpu.CompilerParams(vmem_limit_bytes=40 * 2**20),
        cost_estimate=pl.CostEstimate(
            flops=int(micros * 1e9), bytes_accessed=0, transcendentals=0
        ),
    )(*operands)


def local(
    ket, corner_tl, corner_tr, corner_bl, edge_left, edge_top, edge_right, edge_bottom,
    row_sketch, col_sketch,
):
    squeeze = lambda value: value.reshape(value.shape[2:])
    legs_first = lambda value: jnp.swapaxes(squeeze(value), 0, 1)
    ket, corner_tl, corner_tr, corner_bl = map(squeeze, (ket, corner_tl, corner_tr, corner_bl))
    edge_left, edge_top, edge_right, edge_bottom = map(
        legs_first, (edge_left, edge_top, edge_right, edge_bottom)
    )
    row_sketch, col_sketch = map(squeeze, (row_sketch, col_sketch))
    legs, chi, _ = edge_left.shape
    bond = round(legs**0.5)
    size = padded(legs * legs, 32)
    flat = (chi, legs * chi)
    main = (chi * MAIN, chi)
    square = (chi, chi)
    pair_of = (chi, 2 * chi)
    site = (size, size)
    moved = (chi, (legs + 2) * chi)
    passed_main = (chi * MAIN, legs * chi)
    passed_tails = (legs - MAIN, chi, legs * chi)
    tmp = pltpu.VMEM((chi * legs, chi), F32)
    side = pltpu.VMEM((padded((legs - MAIN) * legs, MAIN) * chi, chi), F32)
    short = lambda value: pltpu.VMEM(value, BF16)

    forth, back = kernel_call(
        functools.partial(site_kernel, bond=bond, legs=legs), 10, [site, site], [], ket
    )
    lower, bottom_pair, left_main = kernel_call(
        lower_kernel, 20, [flat, flat, main], [tmp, side],
        corner_bl, edge_bottom, edge_left, row_sketch, back,
    )
    lower_next = lax.ppermute(lower, "row", ring("row", -1))
    upper, top_pair = kernel_call(
        upper_kernel, 20, [flat, flat], [tmp, side],
        corner_tl, edge_top, left_main, edge_left, row_sketch, forth,
    )
    upper_before = lax.ppermute(upper, "row", ring("row", 1))
    right, right_pair, top_main = kernel_call(
        right_kernel, 0.02, [flat, flat, main], [tmp, side],
        corner_tr, edge_right, edge_top, col_sketch, forth,
    )
    right_next = lax.ppermute(right, "col", ring("col", -1))
    lower_next, right = lax.optimization_barrier((lower_next, right))
    passed, tails = kernel_call(
        pass_kernel, 0.02, [passed_main, passed_tails], [side],
        upper, lower_next, left_main, edge_left, back,
    )
    (moved_left,) = kernel_call(
        left_move_kernel, 0.02, [moved], [tmp],
        upper, lower_next, upper_before, lower, top_pair, bottom_pair, passed, tails,
    )
    right_next, moved_left = lax.optimization_barrier((right_next, moved_left))
    moved_left = lax.ppermute(moved_left, "col", ring("col", 1))
    edge_left_new, corner_bl_new, term, left_pair = kernel_call(
        left_cut_kernel, 0.02, [edge_left.shape, square, flat, flat],
        [tmp, side, pltpu.SemaphoreType.DMA((legs + 1,))],
        moved_left, top_main, edge_top, back, col_sketch, stores=2,
    )
    term_before = lax.ppermute(term, "col", ring("col", 1))
    inverse, right_up = kernel_call(
        inverse_kernel, 0.02, [pair_of, square], [], term, right_next, right_pair
    )
    west = lax.ppermute(inverse, ("row", "col"), diagonal())
    right_next, inverse = lax.optimization_barrier((right_next, inverse))
    passed, tails = kernel_call(
        pass_kernel, 0.02, [passed_main, passed_tails], [side],
        term, right_next, top_main, edge_top, forth,
    )
    term_before, passed = lax.optimization_barrier((term_before, passed))
    (moved_up,) = kernel_call(
        up_move_kernel, 0.02, [moved], [tmp],
        term_before, right, left_pair, passed, tails, inverse, right_up,
    )
    moved_up = lax.ppermute(moved_up, "row", ring("row", 1))
    edge_top_new, corner_tl_new, corner_tr_new = kernel_call(
        finish_kernel, 0.02, [edge_top.shape, square, square],
        [short(edge_top.shape), short(square), pltpu.SemaphoreType.DMA((3,))],
        moved_up, west, stores=3,
    )
    outs = (
        jnp.swapaxes(edge_left_new, 0, 1), corner_bl_new,
        jnp.swapaxes(edge_top_new, 0, 1), corner_tl_new, corner_tr_new,
    )
    return tuple(value.reshape((1, 1) + value.shape) for value in outs)


def solution(mesh):
    matrix = P("row", "col", None, None)
    tensor = P("row", "col", None, None, None)
    return jax.shard_map(
        local,
        mesh=mesh,
        in_specs=(matrix,) * 4 + (tensor,) * 6,
        out_specs=(tensor, matrix, tensor, matrix, matrix),
        check_vma=False,
    )
```

```python
import functools

import jax
import jax.numpy as jnp
from jax import lax
from jax.experimental import pallas as pl
from jax.experimental.pallas import tpu as pltpu
from jax.sharding import PartitionSpec as P

NS_STEPS = 8
MAIN = 8
F32 = jnp.float32
BF16 = jnp.bfloat16
HIGHEST = lax.Precision.HIGHEST


def ring(axis, steps):
    count = lax.axis_size(axis)
    return [(source, (source + steps) % count) for source in range(count)]


def diagonal():
    rows, cols = lax.axis_size("row"), lax.axis_size("col")
    return [
        (row * cols + col, (row + 1) % rows * cols + (col + 1) % cols)
        for row in range(rows)
        for col in range(cols)
    ]


def padded(count, multiple):
    return -(-count // multiple) * multiple


def mul(former, latter):
    return jnp.dot(former, latter, preferred_element_type=F32)


def mul_first(former, latter):
    return lax.dot_general(former, latter, (((0,), (0,)), ((), ())), preferred_element_type=F32)


def beside(parts):
    return jnp.concatenate(parts, axis=1)


def under(parts):
    return jnp.concatenate(parts, axis=0)


def legs_of_flat(flat, chi):
    return [flat[:, start : start + chi] for start in range(0, flat.shape[1], chi)]


def legs_of_first(ref):
    return [ref[leg] for leg in range(ref.shape[0])]


def legs_of_rows(rows, tmp, legs):
    count = rows.shape[0]
    tmp[:count, :] = rows.astype(F32)
    return [
        tmp[pl.ds(leg, count // legs, stride=legs), :].astype(BF16) for leg in range(legs)
    ]


def main_of_legs(parts, tmp):
    chi = parts[0].shape[0]
    for leg in range(MAIN):
        tmp[pl.ds(leg, chi, stride=MAIN), :] = parts[leg].astype(F32)
    return tmp[: chi * MAIN, :].astype(BF16)


def pass_site(main, tails, flat, matrix, sides):
    chi = tails[0].shape[0]
    legs = flat.shape[1] // chi
    size = matrix.shape[0]
    first = legs * MAIN
    used = len(tails) * legs
    rows = padded(used, MAIN)
    side, side_out = sides.at[0], sides.at[1]
    for index, tail in enumerate(tails):
        for leg, part in enumerate(legs_of_flat(mul(tail, flat), chi)):
            here = (index * legs + leg) * chi
            side[here : here + chi, :] = part
    side[used * chi : rows * chi, :] = jnp.zeros(((rows - used) * chi, chi), F32)
    block = mul(main, flat)
    fill = [jnp.zeros((size - first - rows, chi), F32)] if size > first + rows else []
    columns = beside(
        [
            under(
                legs_of_flat(block[one * MAIN : (one + 1) * MAIN, :], chi)
                + [side[pl.ds(one, rows, stride=chi), :]]
                + fill
            ).astype(BF16)
            for one in range(chi)
        ]
    )
    passed = mul(matrix, columns)
    out = []
    for one in range(chi):
        here = passed[:, one * chi : (one + 1) * chi]
        out.append(beside([here[leg * MAIN : (leg + 1) * MAIN] for leg in range(legs)]))
        side_out[pl.ds(one, rows, stride=chi), :] = here[first : first + rows]
    out_tails = [
        beside(
            [
                side_out[(index * legs + leg) * chi : (index * legs + leg + 1) * chi, :]
                for leg in range(legs)
            ]
        ).astype(BF16)
        for index in range(len(tails))
    ]
    return under(out).astype(BF16), out_tails


def fold(end_main, end_tails, main, tails):
    total = mul_first(end_main, main)
    for end, tail in zip(end_tails, tails):
        total = total + mul_first(end, tail)
    return total


def spread(main, tails, end, tmp):
    chi = tails[0].shape[0]
    tmp[: chi * MAIN, :] = mul(main, end)
    parts = [tmp[pl.ds(leg, chi, stride=MAIN), :] for leg in range(MAIN)]
    return beside(parts + [mul(tail, end) for tail in tails])


def rescaled(value):
    return (value * lax.rsqrt(jnp.mean(value * value) + 1e-06)).astype(BF16)


def split(value):
    high = value.astype(BF16)
    return high, (value - high.astype(F32)).astype(BF16)


def mul_split(former, latter):
    (high, low), (other_high, other_low) = former, latter
    return mul(beside([high, low]), under([other_high, other_high])) + mul(high, other_low)


def inverse_roots(grams, pieces=()):
    pieces = list(pieces)
    step = lambda: pieces.pop(0)() if pieces else None
    chi = grams[0].shape[0]
    rows = lax.broadcasted_iota(jnp.int32, (chi, chi), 0)
    columns = lax.broadcasted_iota(jnp.int32, (chi, chi), 1)
    identity = jnp.where(rows == columns, 1.0, 0.0).astype(F32)
    scalings = [jnp.sum(gram * identity) + 1e-06 for gram in grams]
    currents = [gram / scaling for gram, scaling in zip(grams, scalings)]
    inverses = [1.5 * identity - 0.5 * current for current in currents]
    currents = [
        mul_split(split(current), split(inverse))
        for current, inverse in zip(currents, inverses)
    ]
    step()
    for iteration in range(1, NS_STEPS):
        nows = [split(current) for current in currents]
        invs = [split(inverse) for inverse in inverses]
        factors = [
            split(1.5 * identity - 0.5 * mul_split(inv, now)) for inv, now in zip(invs, nows)
        ]
        step()
        if iteration < NS_STEPS - 1:
            boths = [
                mul_split(factor, (beside([now[0], inv[0]]), beside([now[1], inv[1]])))
                for factor, now, inv in zip(factors, nows, invs)
            ]
            currents = [both[:, :chi] for both in boths]
            inverses = [both[:, chi:] for both in boths]
        else:
            inverses = [mul_split(factor, inv) for factor, inv in zip(factors, invs)]
        step()
    while pieces:
        step()
    return [
        beside(split(inverse * lax.rsqrt(scaling)))
        for inverse, scaling in zip(inverses, scalings)
    ]


def site_picks(bond, legs, size):
    shape = (size, bond**4)
    row = lax.broadcasted_iota(jnp.int32, shape, 0)
    column = lax.broadcasted_iota(jnp.int32, shape, 1)
    digit = lambda value, place: lax.rem(lax.div(value, bond**place), bond)
    late = row - legs * MAIN
    first = jnp.where(late < 0, lax.div(row, MAIN), lax.rem(jnp.maximum(late, 0), legs))
    second = jnp.where(
        late < 0, lax.rem(row, MAIN), MAIN + lax.div(jnp.maximum(late, 0), legs)
    )
    up, left, down, right = (digit(column, place) for place in (3, 2, 1, 0))
    picks = []
    for one, two in ((down, left), (right, up)):
        for place in (1, 0):
            hit = (digit(first, place) == one) & (digit(second, place) == two)
            picks.append(jnp.where(hit & (row < legs * legs), 1.0, 0.0).astype(F32))
    return picks


def site_kernel(ket_ref, forth_ref, back_ref, *, bond, legs):
    picks = site_picks(bond, legs, forth_ref.shape[0])
    forth = 0.0
    back = 0.0
    for phys in range(ket_ref.shape[0]):
        row = ket_ref[pl.ds(phys, 1), :]
        factors = []
        for first, second in ((0, 2), (2, 0)):
            for layer in range(2):
                factors.append(
                    lax.dot_general(
                        picks[first + layer] * row, picks[second + layer],
                        (((1,), (1,)), ((), ())), precision=HIGHEST, preferred_element_type=F32,
                    )
                )
        forth = forth + factors[0] * factors[1]
        back = back + factors[2] * factors[3]
    forth_ref[...] = forth.astype(BF16)
    back_ref[...] = back.astype(BF16)


def lower_kernel(
    corner_ref, bottom_ref, left_ref, sketch_ref, back_ref,
    lower_ref, pair_ref, left_main_ref, tmp, side,
):
    legs = left_ref.shape[0]
    left = legs_of_first(left_ref)
    left_main_ref[...] = main_of_legs(left, tmp)
    pair = mul(corner_ref[...], beside(legs_of_first(bottom_ref))).astype(BF16)
    pair_ref[...] = pair
    folded = under(legs_of_rows(sketch_ref[1], tmp, legs))
    passed, tails = pass_site(left_main_ref[...], left[MAIN:], pair, back_ref[...], side)
    lower_ref[...] = spread(passed, tails, folded, tmp).astype(BF16)


def right_kernel(
    corner_ref, edge_ref, top_ref, sketch_ref, forth_ref,
    right_ref, pair_ref, top_main_ref, tmp, side,
):
    legs = edge_ref.shape[0]
    top = legs_of_first(top_ref)
    top_main_ref[...] = main_of_legs(top, tmp)
    pair = mul(corner_ref[...], beside(legs_of_first(edge_ref))).astype(BF16)
    pair_ref[...] = pair
    folded = under(legs_of_rows(sketch_ref[1], tmp, legs))
    passed, tails = pass_site(top_main_ref[...], top[MAIN:], pair, forth_ref[...], side)
    right_ref[...] = spread(passed, tails, folded, tmp).astype(BF16)


def upper_kernel(
    corner_ref, top_ref, left_main_ref, left_ref, sketch_ref, forth_ref,
    upper_ref, pair_ref, tmp, side,
):
    legs, chi, _ = left_ref.shape
    pair = mul_first(corner_ref[...], beside(legs_of_first(top_ref))).astype(BF16)
    pair_ref[...] = pair
    parts = legs_of_flat(pair, chi)
    sketch = beside(legs_of_rows(sketch_ref[0], tmp, legs))
    main = main_of_legs(parts, tmp)
    passed, tails = pass_site(main, parts[MAIN:], sketch, forth_ref[...], side)
    ends = legs_of_first(left_ref)[MAIN:]
    upper_ref[...] = fold(left_main_ref[...], ends, passed, tails).astype(BF16)


def cut_legs(former_ref, latter_ref):
    chi = former_ref.shape[0]
    cut = former_ref[...].astype(F32) + latter_ref[...].astype(F32)
    return legs_of_flat(cut.astype(BF16), chi)


def halves(value):
    chi = value.shape[1] // 2
    return value[:, :chi] + value[:, chi:]


def right_times(value, inverse):
    return halves(mul(value, inverse))


def left_times(inverse, value):
    chi = inverse.shape[0]
    both = mul_first(inverse, value)
    return both[:chi] + both[chi:]


def inverse_kernel(former_ref, latter_ref, pair_ref, inverse_ref, corner_ref):
    cut = under(cut_legs(former_ref, latter_ref))
    pair = under(legs_of_flat(pair_ref[...], former_ref.shape[0]))
    (inverse,) = inverse_roots([mul_first(cut, cut)])
    inverse_ref[...] = inverse
    corner_ref[...] = rescaled(left_times(inverse, mul_first(cut, pair).astype(BF16)))


def pass_kernel(
    former_ref, latter_ref, main_ref, edge_ref, matrix_ref, passed_ref, tails_ref, side
):
    cut = cut_legs(former_ref, latter_ref)
    passed, tails = pass_site(
        main_ref[...], legs_of_first(edge_ref)[MAIN:], beside(cut), matrix_ref[...], side
    )
    passed_ref[...] = passed
    for index, tail in enumerate(tails):
        tails_ref[index] = tail


def folded_cut(cut, passed_ref, tails_ref, tmp):
    tails = [tails_ref[index] for index in range(tails_ref.shape[0])]
    return fold(main_of_legs(cut, tmp), cut[MAIN:], passed_ref[...], tails).astype(BF16)


def left_move_kernel(
    upper_ref, lower_next_ref, upper_before_ref, lower_ref, top_pair_ref, bottom_pair_ref,
    passed_ref, tails_ref, moved_ref, tmp,
):
    chi = upper_ref.shape[0]
    below = cut_legs(upper_ref, lower_next_ref)
    above = cut_legs(upper_before_ref, lower_ref)
    rows_below, rows_above = under(below), under(above)
    grams = [mul_first(rows_below, rows_below), mul_first(rows_above, rows_above)]
    corners = []
    edge = []
    main = main_of_legs(above, tmp).T
    tails = [(end.T, tails_ref[index]) for index, end in enumerate(above[MAIN:])]

    def top_piece():
        pair = under(legs_of_flat(top_pair_ref[...], chi))
        corners.append(mul_first(pair, rows_above).astype(BF16))

    def bottom_piece():
        pair = under(legs_of_flat(bottom_pair_ref[...], chi))
        corners.append(mul_first(rows_below, pair).astype(BF16))

    def edge_piece(start):
        here = slice(start, start + chi)
        part = mul(main, passed_ref[:, here])
        for end, tail in tails:
            part = part + mul(end, tail[:, here])
        edge.append(part.astype(BF16))

    pieces = [top_piece, bottom_piece]
    pieces += [functools.partial(edge_piece, at) for at in range(0, passed_ref.shape[1], chi)]
    inverse_below, inverse_above = inverse_roots(grams, pieces)
    top, bottom = corners
    edge = beside(edge)
    turned = left_times(inverse_above, edge).astype(BF16)
    rows = rescaled(right_times(under(legs_of_flat(turned, chi)), inverse_below))
    moved_ref[...] = beside(
        [rows[start : start + chi] for start in range(0, rows.shape[0], chi)]
        + [
            rescaled(right_times(top, inverse_above)),
            rescaled(left_times(inverse_below, bottom)),
        ]
    )


def sketch_kernel(sketch_ref, flat_ref, tmp):
    legs = flat_ref.shape[1] // flat_ref.shape[0]
    flat_ref[...] = beside(legs_of_rows(sketch_ref[0], tmp, legs))


def left_cut_kernel(
    moved_ref, top_main_ref, top_ref, back_ref, sketch_ref,
    edge_ref, bottom_ref, term_ref, pair_ref, tmp, side, sems,
):
    legs, chi, _ = top_ref.shape
    part = lambda leg: moved_ref.at[:, leg * chi : (leg + 1) * chi]
    outs = [edge_ref.at[leg] for leg in range(legs)]
    stores = [pltpu.make_async_copy(part(leg), outs[leg], sems.at[leg]) for leg in range(legs)]
    stores.append(pltpu.make_async_copy(part(legs + 1), bottom_ref, sems.at[legs]))
    for store in stores:
        store.start()
    corner = moved_ref[:, legs * chi : (legs + 1) * chi]
    pair = mul(corner, moved_ref[:, : legs * chi]).astype(BF16)
    pair_ref[...] = pair
    parts = legs_of_flat(pair, chi)
    main = main_of_legs(parts, tmp)
    passed, tails = pass_site(main, parts[MAIN:], sketch_ref[...], back_ref[...], side)
    ends = legs_of_first(top_ref)[MAIN:]
    term_ref[...] = fold(top_main_ref[...], ends, passed, tails).astype(BF16)
    for store in stores:
        store.wait()


def up_move_kernel(
    term_before_ref, right_ref, left_pair_ref, passed_ref, tails_ref, inverse_ref, corner_ref,
    moved_ref, tmp,
):
    chi = right_ref.shape[0]
    west = cut_legs(term_before_ref, right_ref)
    left = mul_first(under(west), under(legs_of_flat(left_pair_ref[...], chi)))
    edge = under(legs_of_flat(folded_cut(west, passed_ref, tails_ref, tmp), chi))
    rows = right_times(edge, inverse_ref[...]).astype(BF16)
    moved_ref[...] = beside(
        [rows[start : start + chi] for start in range(0, rows.shape[0], chi)]
        + [left.astype(BF16), corner_ref[...]]
    )


def finish_kernel(
    moved_ref, west_ref, edge_ref, left_ref, right_ref, edge, left, sems
):
    legs, chi, _ = edge.shape
    stores = [
        pltpu.make_async_copy(moved_ref.at[:, (legs + 1) * chi :], right_ref, sems.at[0])
    ]
    stores[0].start()
    both = left_times(west_ref[...], moved_ref[:, : (legs + 1) * chi])
    left[...] = rescaled(both[:, legs * chi :])
    stores.append(pltpu.make_async_copy(left, left_ref, sems.at[1]))
    stores[1].start()
    flat = rescaled(both[:, : legs * chi])
    for leg, part in enumerate(legs_of_flat(flat, chi)):
        edge[leg] = part
    stores.append(pltpu.make_async_copy(edge, edge_ref, sems.at[2]))
    stores[2].start()
    for store in stores:
        store.wait()


def kernel_call(kernel, micros, outs, scratch, *operands, stores=0):
    place = lambda own: pl.BlockSpec(memory_space=pltpu.HBM if own else pltpu.VMEM)
    return pl.pallas_call(
        kernel,
        out_shape=[jax.ShapeDtypeStruct(shape, BF16) for shape in outs],
        in_specs=[place(False)] * len(operands),
        out_specs=[place(index < stores) for index in range(len(outs))],
        scratch_shapes=scratch,
        compiler_params=pltpu.CompilerParams(vmem_limit_bytes=40 * 2**20),
        cost_estimate=pl.CostEstimate(
            flops=int(micros * 1e9), bytes_accessed=0, transcendentals=0
        ),
    )(*operands)


def local(
    ket, corner_tl, corner_tr, corner_bl, edge_left, edge_top, edge_right, edge_bottom,
    row_sketch, col_sketch,
):
    squeeze = lambda value: value.reshape(value.shape[2:])
    legs_first = lambda value: jnp.swapaxes(squeeze(value), 0, 1)
    ket, corner_tl, corner_tr, corner_bl = map(squeeze, (ket, corner_tl, corner_tr, corner_bl))
    edge_left, edge_top, edge_right, edge_bottom = map(
        legs_first, (edge_left, edge_top, edge_right, edge_bottom)
    )
    row_sketch, col_sketch = map(squeeze, (row_sketch, col_sketch))
    legs, chi, _ = edge_left.shape
    bond = round(legs**0.5)
    size = padded(legs * legs, 32)
    flat = (chi, legs * chi)
    main = (chi * MAIN, chi)
    square = (chi, chi)
    pair_of = (chi, 2 * chi)
    site = (size, size)
    moved = (chi, (legs + 2) * chi)
    passed_main = (chi * MAIN, legs * chi)
    passed_tails = (legs - MAIN, chi, legs * chi)
    tmp = pltpu.VMEM((chi * legs, chi), F32)
    side = pltpu.VMEM((2, padded((legs - MAIN) * legs, MAIN) * chi, chi), F32)
    short = lambda value: pltpu.VMEM(value, BF16)

    forth, back = kernel_call(
        functools.partial(site_kernel, bond=bond, legs=legs), 10, [site, site], [], ket
    )
    lower, bottom_pair, left_main = kernel_call(
        lower_kernel, 20, [flat, flat, main], [tmp, side],
        corner_bl, edge_bottom, edge_left, row_sketch, back,
    )
    lower_next = lax.ppermute(lower, "row", ring("row", -1))
    upper, top_pair = kernel_call(
        upper_kernel, 20, [flat, flat], [tmp, side],
        corner_tl, edge_top, left_main, edge_left, row_sketch, forth,
    )
    upper_before = lax.ppermute(upper, "row", ring("row", 1))
    right, right_pair, top_main = kernel_call(
        right_kernel, 0.02, [flat, flat, main], [tmp, side],
        corner_tr, edge_right, edge_top, col_sketch, forth,
    )
    right_next = lax.ppermute(right, "col", ring("col", -1))
    lower_next, right = lax.optimization_barrier((lower_next, right))
    passed, tails = kernel_call(
        pass_kernel, 0.02, [passed_main, passed_tails], [side],
        upper, lower_next, left_main, edge_left, back,
    )
    (moved_left,) = kernel_call(
        left_move_kernel, 0.02, [moved], [tmp],
        upper, lower_next, upper_before, lower, top_pair, bottom_pair, passed, tails,
    )
    moved_left = lax.ppermute(moved_left, "col", ring("col", 1))
    (left_sketch,) = kernel_call(sketch_kernel, 0.02, [flat], [tmp], col_sketch)
    edge_left_new, corner_bl_new, term, left_pair = kernel_call(
        left_cut_kernel, 0.02, [edge_left.shape, square, flat, flat],
        [tmp, side, pltpu.SemaphoreType.DMA((legs + 1,))],
        moved_left, top_main, edge_top, back, left_sketch, stores=2,
    )
    term_before = lax.ppermute(term, "col", ring("col", 1))
    inverse, right_up = kernel_call(
        inverse_kernel, 0.02, [pair_of, square], [], term, right_next, right_pair
    )
    west = lax.ppermute(inverse, ("row", "col"), diagonal())
    right_next, inverse = lax.optimization_barrier((right_next, inverse))
    passed, tails = kernel_call(
        pass_kernel, 0.02, [passed_main, passed_tails], [side],
        term, right_next, top_main, edge_top, forth,
    )
    term_before, passed = lax.optimization_barrier((term_before, passed))
    (moved_up,) = kernel_call(
        up_move_kernel, 0.02, [moved], [tmp],
        term_before, right, left_pair, passed, tails, inverse, right_up,
    )
    moved_up = lax.ppermute(moved_up, "row", ring("row", 1))
    edge_top_new, corner_tl_new, corner_tr_new = kernel_call(
        finish_kernel, 0.02, [edge_top.shape, square, square],
        [short(edge_top.shape), short(square), pltpu.SemaphoreType.DMA((3,))],
        moved_up, west, stores=3,
    )
    outs = (
        jnp.swapaxes(edge_left_new, 0, 1), corner_bl_new,
        jnp.swapaxes(edge_top_new, 0, 1), corner_tl_new, corner_tr_new,
    )
    return tuple(value.reshape((1, 1) + value.shape) for value in outs)


def solution(mesh):
    matrix = P("row", "col", None, None)
    tensor = P("row", "col", None, None, None)
    return jax.shard_map(
        local,
        mesh=mesh,
        in_specs=(matrix,) * 4 + (tensor,) * 6,
        out_specs=(tensor, matrix, tensor, matrix, matrix),
        check_vma=False,
    )
```

```python
import functools

import jax
import jax.numpy as jnp
from jax import lax
from jax.experimental import pallas as pl
from jax.experimental.pallas import tpu as pltpu
from jax.sharding import PartitionSpec as P

NS_STEPS = 8
MAIN = 8
F32 = jnp.float32
BF16 = jnp.bfloat16
HIGHEST = lax.Precision.HIGHEST


def ring(axis, steps):
    count = lax.axis_size(axis)
    return [(source, (source + steps) % count) for source in range(count)]


def diagonal():
    rows, cols = lax.axis_size("row"), lax.axis_size("col")
    return [
        (row * cols + col, (row + 1) % rows * cols + (col + 1) % cols)
        for row in range(rows)
        for col in range(cols)
    ]


def padded(count, multiple):
    return -(-count // multiple) * multiple


def mul(former, latter):
    return jnp.dot(former, latter, preferred_element_type=F32)


def mul_first(former, latter):
    return lax.dot_general(former, latter, (((0,), (0,)), ((), ())), preferred_element_type=F32)


def beside(parts):
    return jnp.concatenate(parts, axis=1)


def under(parts):
    return jnp.concatenate(parts, axis=0)


def legs_of_flat(flat, chi):
    return [flat[:, start : start + chi] for start in range(0, flat.shape[1], chi)]


def legs_of_first(ref):
    return [ref[leg] for leg in range(ref.shape[0])]


def legs_of_rows(rows, tmp, legs):
    count = rows.shape[0]
    tmp[:count, :] = rows.astype(F32)
    return [
        tmp[pl.ds(leg, count // legs, stride=legs), :].astype(BF16) for leg in range(legs)
    ]


def main_of_legs(parts, tmp):
    chi = parts[0].shape[0]
    for leg in range(MAIN):
        tmp[pl.ds(leg, chi, stride=MAIN), :] = parts[leg].astype(F32)
    return tmp[: chi * MAIN, :].astype(BF16)


def pass_site(main, tails, flat, matrix, sides):
    chi = tails[0].shape[0]
    legs = flat.shape[1] // chi
    size = matrix.shape[0]
    first = legs * MAIN
    used = len(tails) * legs
    rows = padded(used, MAIN)
    side, side_out = sides.at[0], sides.at[1]
    for index, tail in enumerate(tails):
        for leg, part in enumerate(legs_of_flat(mul(tail, flat), chi)):
            here = (index * legs + leg) * chi
            side[here : here + chi, :] = part
    side[used * chi : rows * chi, :] = jnp.zeros(((rows - used) * chi, chi), F32)
    block = mul(main, flat)
    fill = [jnp.zeros((size - first - rows, chi), F32)] if size > first + rows else []
    columns = beside(
        [
            under(
                legs_of_flat(block[one * MAIN : (one + 1) * MAIN, :], chi)
                + [side[pl.ds(one, rows, stride=chi), :]]
                + fill
            ).astype(BF16)
            for one in range(chi)
        ]
    )
    passed = mul(matrix, columns)
    out = []
    for one in range(chi):
        here = passed[:, one * chi : (one + 1) * chi]
        out.append(beside([here[leg * MAIN : (leg + 1) * MAIN] for leg in range(legs)]))
        side_out[pl.ds(one, rows, stride=chi), :] = here[first : first + rows]
    out_tails = [
        beside(
            [
                side_out[(index * legs + leg) * chi : (index * legs + leg + 1) * chi, :]
                for leg in range(legs)
            ]
        ).astype(BF16)
        for index in range(len(tails))
    ]
    return under(out).astype(BF16), out_tails


def fold(end_main, end_tails, main, tails):
    total = mul_first(end_main, main)
    for end, tail in zip(end_tails, tails):
        total = total + mul_first(end, tail)
    return total


def spread(main, tails, end, tmp):
    chi = tails[0].shape[0]
    tmp[: chi * MAIN, :] = mul(main, end)
    parts = [tmp[pl.ds(leg, chi, stride=MAIN), :] for leg in range(MAIN)]
    return beside(parts + [mul(tail, end) for tail in tails])


def rescaled(value):
    return (value * lax.rsqrt(jnp.mean(value * value) + 1e-06)).astype(BF16)


def split(value):
    high = value.astype(BF16)
    return high, (value - high.astype(F32)).astype(BF16)


def mul_split(former, latter):
    (high, low), (other_high, other_low) = former, latter
    return mul(beside([high, low]), under([other_high, other_high])) + mul(high, other_low)


def inverse_roots(grams, pieces=()):
    pieces = list(pieces)
    step = lambda: pieces.pop(0)() if pieces else None
    chi = grams[0].shape[0]
    rows = lax.broadcasted_iota(jnp.int32, (chi, chi), 0)
    columns = lax.broadcasted_iota(jnp.int32, (chi, chi), 1)
    identity = jnp.where(rows == columns, 1.0, 0.0).astype(F32)
    scalings = [jnp.sum(gram * identity) + 1e-06 for gram in grams]
    currents = [gram / scaling for gram, scaling in zip(grams, scalings)]
    inverses = [1.5 * identity - 0.5 * current for current in currents]
    currents = [
        mul_split(split(current), split(inverse))
        for current, inverse in zip(currents, inverses)
    ]
    step()
    for iteration in range(1, NS_STEPS):
        nows = [split(current) for current in currents]
        invs = [split(inverse) for inverse in inverses]
        factors = [
            split(1.5 * identity - 0.5 * mul_split(inv, now)) for inv, now in zip(invs, nows)
        ]
        step()
        if iteration < NS_STEPS - 1:
            boths = [
                mul_split(factor, (beside([now[0], inv[0]]), beside([now[1], inv[1]])))
                for factor, now, inv in zip(factors, nows, invs)
            ]
            currents = [both[:, :chi] for both in boths]
            inverses = [both[:, chi:] for both in boths]
        else:
            inverses = [mul_split(factor, inv) for factor, inv in zip(factors, invs)]
        step()
    while pieces:
        step()
    return [
        beside(split(inverse * lax.rsqrt(scaling)))
        for inverse, scaling in zip(inverses, scalings)
    ]


def site_picks(bond, legs, size):
    shape = (size, bond**4)
    row = lax.broadcasted_iota(jnp.int32, shape, 0)
    column = lax.broadcasted_iota(jnp.int32, shape, 1)
    digit = lambda value, place: lax.rem(lax.div(value, bond**place), bond)
    late = row - legs * MAIN
    first = jnp.where(late < 0, lax.div(row, MAIN), lax.rem(jnp.maximum(late, 0), legs))
    second = jnp.where(
        late < 0, lax.rem(row, MAIN), MAIN + lax.div(jnp.maximum(late, 0), legs)
    )
    up, left, down, right = (digit(column, place) for place in (3, 2, 1, 0))
    picks = []
    for one, two in ((down, left), (right, up)):
        for place in (1, 0):
            hit = (digit(first, place) == one) & (digit(second, place) == two)
            picks.append(jnp.where(hit & (row < legs * legs), 1.0, 0.0).astype(F32))
    return picks


def site_kernel(ket_ref, forth_ref, back_ref, *, bond, legs):
    picks = site_picks(bond, legs, forth_ref.shape[0])
    forth = 0.0
    back = 0.0
    for phys in range(ket_ref.shape[0]):
        row = ket_ref[pl.ds(phys, 1), :]
        factors = []
        for first, second in ((0, 2), (2, 0)):
            for layer in range(2):
                factors.append(
                    lax.dot_general(
                        picks[first + layer] * row, picks[second + layer],
                        (((1,), (1,)), ((), ())), precision=HIGHEST, preferred_element_type=F32,
                    )
                )
        forth = forth + factors[0] * factors[1]
        back = back + factors[2] * factors[3]
    forth_ref[...] = forth.astype(BF16)
    back_ref[...] = back.astype(BF16)


def lower_kernel(
    corner_ref, bottom_ref, left_ref, sketch_ref, back_ref,
    lower_ref, pair_ref, left_main_ref, tmp, side,
):
    legs = left_ref.shape[0]
    left = legs_of_first(left_ref)
    left_main_ref[...] = main_of_legs(left, tmp)
    pair = mul(corner_ref[...], beside(legs_of_first(bottom_ref))).astype(BF16)
    pair_ref[...] = pair
    folded = under(legs_of_rows(sketch_ref[1], tmp, legs))
    passed, tails = pass_site(left_main_ref[...], left[MAIN:], pair, back_ref[...], side)
    lower_ref[...] = spread(passed, tails, folded, tmp).astype(BF16)


def right_kernel(
    corner_ref, edge_ref, top_ref, sketch_ref, forth_ref,
    upper_ref, lower_next_ref, bottom_pair_ref, inverse_ref,
    right_ref, pair_ref, top_main_ref, left_sketch_ref, bottom_ref, tmp, side,
):
    chi = upper_ref.shape[0]
    cut = under(cut_legs(upper_ref, lower_next_ref))
    corner = mul_first(cut, under(legs_of_flat(bottom_pair_ref[...], chi))).astype(BF16)
    bottom_ref[...] = rescaled(left_times(inverse_ref[...], corner))
    legs = edge_ref.shape[0]
    top = legs_of_first(top_ref)
    top_main_ref[...] = main_of_legs(top, tmp)
    pair = mul(corner_ref[...], beside(legs_of_first(edge_ref))).astype(BF16)
    pair_ref[...] = pair
    left_sketch_ref[...] = beside(legs_of_rows(sketch_ref[0], tmp, legs))
    folded = under(legs_of_rows(sketch_ref[1], tmp, legs))
    passed, tails = pass_site(top_main_ref[...], top[MAIN:], pair, forth_ref[...], side)
    right_ref[...] = spread(passed, tails, folded, tmp).astype(BF16)


def upper_kernel(
    corner_ref, top_ref, left_main_ref, left_ref, sketch_ref, forth_ref,
    upper_ref, pair_ref, tmp, side,
):
    legs, chi, _ = left_ref.shape
    pair = mul_first(corner_ref[...], beside(legs_of_first(top_ref))).astype(BF16)
    pair_ref[...] = pair
    parts = legs_of_flat(pair, chi)
    sketch = beside(legs_of_rows(sketch_ref[0], tmp, legs))
    main = main_of_legs(parts, tmp)
    passed, tails = pass_site(main, parts[MAIN:], sketch, forth_ref[...], side)
    ends = legs_of_first(left_ref)[MAIN:]
    upper_ref[...] = fold(left_main_ref[...], ends, passed, tails).astype(BF16)


def cut_legs(former_ref, latter_ref):
    chi = former_ref.shape[0]
    cut = former_ref[...].astype(F32) + latter_ref[...].astype(F32)
    return legs_of_flat(cut.astype(BF16), chi)


def halves(value):
    chi = value.shape[1] // 2
    return value[:, :chi] + value[:, chi:]


def right_times(value, inverse):
    return halves(mul(value, inverse))


def left_times(inverse, value):
    chi = inverse.shape[0]
    both = mul_first(inverse, value)
    return both[:chi] + both[chi:]


def inverse_kernel(former_ref, latter_ref, pair_ref, inverse_ref, corner_ref):
    cut = under(cut_legs(former_ref, latter_ref))
    pair = under(legs_of_flat(pair_ref[...], former_ref.shape[0]))
    (inverse,) = inverse_roots([mul_first(cut, cut)])
    inverse_ref[...] = inverse
    corner_ref[...] = rescaled(left_times(inverse, mul_first(cut, pair).astype(BF16)))


def pass_kernel(
    former_ref, latter_ref, main_ref, edge_ref, matrix_ref, passed_ref, tails_ref, side
):
    cut = cut_legs(former_ref, latter_ref)
    passed, tails = pass_site(
        main_ref[...], legs_of_first(edge_ref)[MAIN:], beside(cut), matrix_ref[...], side
    )
    passed_ref[...] = passed
    for index, tail in enumerate(tails):
        tails_ref[index] = tail


def folded_cut(cut, passed_ref, tails_ref, tmp):
    tails = [tails_ref[index] for index in range(tails_ref.shape[0])]
    return fold(main_of_legs(cut, tmp), cut[MAIN:], passed_ref[...], tails).astype(BF16)


def left_move_kernel(
    upper_ref, lower_next_ref, upper_before_ref, lower_ref, top_pair_ref,
    passed_ref, tails_ref, moved_ref, inverse_ref, tmp,
):
    chi = upper_ref.shape[0]
    below = cut_legs(upper_ref, lower_next_ref)
    above = cut_legs(upper_before_ref, lower_ref)
    rows_below, rows_above = under(below), under(above)
    grams = [mul_first(rows_below, rows_below), mul_first(rows_above, rows_above)]
    corners = []
    edge = []
    main = main_of_legs(above, tmp).T
    tails = [(end.T, tails_ref[index]) for index, end in enumerate(above[MAIN:])]

    def top_piece():
        pair = under(legs_of_flat(top_pair_ref[...], chi))
        corners.append(mul_first(pair, rows_above).astype(BF16))

    def edge_piece(start):
        here = slice(start, start + chi)
        part = mul(main, passed_ref[:, here])
        for end, tail in tails:
            part = part + mul(end, tail[:, here])
        edge.append(part.astype(BF16))

    pieces = [top_piece]
    pieces += [functools.partial(edge_piece, at) for at in range(0, passed_ref.shape[1], chi)]
    inverse_below, inverse_above = inverse_roots(grams, pieces)
    inverse_ref[...] = inverse_below
    edge = beside(edge)
    turned = left_times(inverse_above, edge).astype(BF16)
    rows = rescaled(right_times(under(legs_of_flat(turned, chi)), inverse_below))
    moved_ref[...] = beside(
        [rows[start : start + chi] for start in range(0, rows.shape[0], chi)]
        + [rescaled(right_times(corners[0], inverse_above))]
    )


def left_cut_kernel(
    moved_ref, top_main_ref, top_ref, back_ref, sketch_ref,
    edge_ref, term_ref, pair_ref, tmp, side, sems,
):
    legs, chi, _ = top_ref.shape
    part = lambda leg: moved_ref.at[:, leg * chi : (leg + 1) * chi]
    outs = [edge_ref.at[leg] for leg in range(legs)]
    stores = [pltpu.make_async_copy(part(leg), outs[leg], sems.at[leg]) for leg in range(legs)]
    for store in stores:
        store.start()
    corner = moved_ref[:, legs * chi : (legs + 1) * chi]
    pair = mul(corner, moved_ref[:, : legs * chi]).astype(BF16)
    pair_ref[...] = pair
    parts = legs_of_flat(pair, chi)
    main = main_of_legs(parts, tmp)
    passed, tails = pass_site(main, parts[MAIN:], sketch_ref[...], back_ref[...], side)
    ends = legs_of_first(top_ref)[MAIN:]
    term_ref[...] = fold(top_main_ref[...], ends, passed, tails).astype(BF16)
    for store in stores:
        store.wait()


def up_move_kernel(
    term_before_ref, right_ref, left_pair_ref, passed_ref, tails_ref, inverse_ref, corner_ref,
    moved_ref, tmp,
):
    chi = right_ref.shape[0]
    west = cut_legs(term_before_ref, right_ref)
    left = mul_first(under(west), under(legs_of_flat(left_pair_ref[...], chi)))
    edge = under(legs_of_flat(folded_cut(west, passed_ref, tails_ref, tmp), chi))
    rows = right_times(edge, inverse_ref[...]).astype(BF16)
    moved_ref[...] = beside(
        [rows[start : start + chi] for start in range(0, rows.shape[0], chi)]
        + [left.astype(BF16), corner_ref[...]]
    )


def finish_kernel(
    moved_ref, west_ref, bottom_ref, edge_ref, left_ref, right_ref, bottom_out_ref,
    edge, left, sems,
):
    legs, chi, _ = edge.shape
    right_part = moved_ref.at[:, (legs + 1) * chi :]
    stores = [
        pltpu.make_async_copy(right_part, right_ref, sems.at[0]),
        pltpu.make_async_copy(bottom_ref, bottom_out_ref, sems.at[3]),
    ]
    for store in stores:
        store.start()
    both = left_times(west_ref[...], moved_ref[:, : (legs + 1) * chi])
    left[...] = rescaled(both[:, legs * chi :])
    stores.append(pltpu.make_async_copy(left, left_ref, sems.at[1]))
    stores[-1].start()
    flat = rescaled(both[:, : legs * chi])
    for leg, part in enumerate(legs_of_flat(flat, chi)):
        edge[leg] = part
    stores.append(pltpu.make_async_copy(edge, edge_ref, sems.at[2]))
    stores[-1].start()
    for store in stores:
        store.wait()


def kernel_call(kernel, micros, outs, scratch, *operands, stores=0):
    place = lambda own: pl.BlockSpec(memory_space=pltpu.HBM if own else pltpu.VMEM)
    return pl.pallas_call(
        kernel,
        out_shape=[jax.ShapeDtypeStruct(shape, BF16) for shape in outs],
        in_specs=[place(False)] * len(operands),
        out_specs=[place(index < stores) for index in range(len(outs))],
        scratch_shapes=scratch,
        compiler_params=pltpu.CompilerParams(vmem_limit_bytes=40 * 2**20),
        cost_estimate=pl.CostEstimate(
            flops=int(micros * 1e9), bytes_accessed=0, transcendentals=0
        ),
    )(*operands)


def local(
    ket, corner_tl, corner_tr, corner_bl, edge_left, edge_top, edge_right, edge_bottom,
    row_sketch, col_sketch,
):
    squeeze = lambda value: value.reshape(value.shape[2:])
    legs_first = lambda value: jnp.swapaxes(squeeze(value), 0, 1)
    ket, corner_tl, corner_tr, corner_bl = map(squeeze, (ket, corner_tl, corner_tr, corner_bl))
    edge_left, edge_top, edge_right, edge_bottom = map(
        legs_first, (edge_left, edge_top, edge_right, edge_bottom)
    )
    row_sketch, col_sketch = map(squeeze, (row_sketch, col_sketch))
    legs, chi, _ = edge_left.shape
    bond = round(legs**0.5)
    size = padded(legs * legs, 32)
    flat = (chi, legs * chi)
    main = (chi * MAIN, chi)
    square = (chi, chi)
    pair_of = (chi, 2 * chi)
    site = (size, size)
    moved_one = (chi, (legs + 1) * chi)
    moved_two = (chi, (legs + 2) * chi)
    passed_main = (chi * MAIN, legs * chi)
    passed_tails = (legs - MAIN, chi, legs * chi)
    tmp = pltpu.VMEM((chi * legs, chi), F32)
    side = pltpu.VMEM((2, padded((legs - MAIN) * legs, MAIN) * chi, chi), F32)
    short = lambda value: pltpu.VMEM(value, BF16)

    forth, back = kernel_call(
        functools.partial(site_kernel, bond=bond, legs=legs), 10, [site, site], [], ket
    )
    lower, bottom_pair, left_main = kernel_call(
        lower_kernel, 20, [flat, flat, main], [tmp, side],
        corner_bl, edge_bottom, edge_left, row_sketch, back,
    )
    lower_next = lax.ppermute(lower, "row", ring("row", -1))
    upper, top_pair = kernel_call(
        upper_kernel, 20, [flat, flat], [tmp, side],
        corner_tl, edge_top, left_main, edge_left, row_sketch, forth,
    )
    upper_before = lax.ppermute(upper, "row", ring("row", 1))
    passed, tails = kernel_call(
        pass_kernel, 0.02, [passed_main, passed_tails], [side],
        upper, lower_next, left_main, edge_left, back,
    )
    moved_left, inverse = kernel_call(
        left_move_kernel, 0.02, [moved_one, pair_of], [tmp],
        upper, lower_next, upper_before, lower, top_pair, passed, tails,
    )
    moved_left, inverse = lax.optimization_barrier((moved_left, inverse))
    moved_left = lax.ppermute(moved_left, "col", ring("col", 1))
    right, right_pair, top_main, left_sketch, bottom_mid = kernel_call(
        right_kernel, 20, [flat, flat, main, flat, square], [tmp, side],
        corner_tr, edge_right, edge_top, col_sketch, forth,
        upper, lower_next, bottom_pair, inverse,
    )
    right_next = lax.ppermute(right, "col", ring("col", -1))
    corner_bl_new = lax.ppermute(bottom_mid, "col", ring("col", 1))
    edge_left_new, term, left_pair = kernel_call(
        left_cut_kernel, 0.02, [edge_left.shape, flat, flat],
        [tmp, side, pltpu.SemaphoreType.DMA((legs,))],
        moved_left, top_main, edge_top, back, left_sketch, stores=1,
    )
    term_before = lax.ppermute(term, "col", ring("col", 1))
    inverse, right_up = kernel_call(
        inverse_kernel, 0.02, [pair_of, square], [], term, right_next, right_pair
    )
    west = lax.ppermute(inverse, ("row", "col"), diagonal())
    right_next, inverse = lax.optimization_barrier((right_next, inverse))
    passed, tails = kernel_call(
        pass_kernel, 0.02, [passed_main, passed_tails], [side],
        term, right_next, top_main, edge_top, forth,
    )
    term_before, passed = lax.optimization_barrier((term_before, passed))
    (moved_up,) = kernel_call(
        up_move_kernel, 0.02, [moved_two], [tmp],
        term_before, right, left_pair, passed, tails, inverse, right_up,
    )
    moved_up = lax.ppermute(moved_up, "row", ring("row", 1))
    edge_top_new, corner_tl_new, corner_tr_new, corner_bl_new = kernel_call(
        finish_kernel, 0.02, [edge_top.shape, square, square, square],
        [short(edge_top.shape), short(square), pltpu.SemaphoreType.DMA((4,))],
        moved_up, west, corner_bl_new, stores=4,
    )
    outs = (
        jnp.swapaxes(edge_left_new, 0, 1), corner_bl_new,
        jnp.swapaxes(edge_top_new, 0, 1), corner_tl_new, corner_tr_new,
    )
    return tuple(value.reshape((1, 1) + value.shape) for value in outs)


def solution(mesh):
    matrix = P("row", "col", None, None)
    tensor = P("row", "col", None, None, None)
    return jax.shard_map(
        local,
        mesh=mesh,
        in_specs=(matrix,) * 4 + (tensor,) * 6,
        out_specs=(tensor, matrix, tensor, matrix, matrix),
        check_vma=False,
    )
```

```python
import functools

import jax
import jax.numpy as jnp
from jax import lax
from jax.experimental import pallas as pl
from jax.experimental.pallas import tpu as pltpu
from jax.sharding import PartitionSpec as P

NS_STEPS = 8
MAIN = 8
F32 = jnp.float32
BF16 = jnp.bfloat16
HIGHEST = lax.Precision.HIGHEST


def ring(axis, steps):
    count = lax.axis_size(axis)
    return [(source, (source + steps) % count) for source in range(count)]


def diagonal():
    rows, cols = lax.axis_size("row"), lax.axis_size("col")
    return [
        (row * cols + col, (row + 1) % rows * cols + (col + 1) % cols)
        for row in range(rows)
        for col in range(cols)
    ]


def padded(count, multiple):
    return -(-count // multiple) * multiple


def mul(former, latter):
    return jnp.dot(former, latter, preferred_element_type=F32)


def mul_first(former, latter):
    return lax.dot_general(former, latter, (((0,), (0,)), ((), ())), preferred_element_type=F32)


def beside(parts):
    return jnp.concatenate(parts, axis=1)


def under(parts):
    return jnp.concatenate(parts, axis=0)


def legs_of_flat(flat, chi):
    return [flat[:, start : start + chi] for start in range(0, flat.shape[1], chi)]


def legs_of_first(ref):
    return [ref[leg] for leg in range(ref.shape[0])]


def legs_of_rows(rows, tmp, legs):
    count = rows.shape[0]
    tmp[:count, :] = rows.astype(F32)
    return [
        tmp[pl.ds(leg, count // legs, stride=legs), :].astype(BF16) for leg in range(legs)
    ]


def main_of_legs(parts, tmp):
    chi = parts[0].shape[0]
    for leg in range(MAIN):
        tmp[pl.ds(leg, chi, stride=MAIN), :] = parts[leg].astype(F32)
    return tmp[: chi * MAIN, :].astype(BF16)


def site_pieces(main, tails, flat, matrix, sides, parts):
    chi = tails[0].shape[0]
    legs = flat.shape[1] // chi
    size = matrix.shape[0]
    first = legs * MAIN
    used = len(tails) * legs
    rows = padded(used, MAIN)
    side, side_out = sides.at[0], sides.at[1]
    fill = [jnp.zeros((size - first - rows, chi), F32)] if size > first + rows else []
    blocks, out = [], []
    share = chi // parts
    halves_of = 2 if parts > 1 else 1

    def start(part):
        here = main[part * share * MAIN : (part + 1) * share * MAIN]
        if part:
            blocks.append(mul(here, flat))
            return
        block = mul(under(tails + [here]), flat)
        for index in range(len(tails)):
            tail = block[index * chi : (index + 1) * chi]
            for leg, value in enumerate(legs_of_flat(tail, chi)):
                at = (index * legs + leg) * chi
                side[at : at + chi, :] = value
        side[used * chi : rows * chi, :] = jnp.zeros(((rows - used) * chi, chi), F32)
        blocks.append(block[len(tails) * chi :])

    def turn(part, half):
        count = share // halves_of
        ones = [half * count + one for one in range(count)]
        columns = beside(
            [
                under(
                    legs_of_flat(blocks[part][one * MAIN : (one + 1) * MAIN, :], chi)
                    + [side[pl.ds(part * share + one, rows, stride=chi), :]]
                    + fill
                ).astype(BF16)
                for one in ones
            ]
        )
        passed = mul(matrix, columns)
        values = []
        for at, one in enumerate(ones):
            here = passed[:, at * chi : (at + 1) * chi]
            values.append(beside([here[leg * MAIN : (leg + 1) * MAIN] for leg in range(legs)]))
            side_out[pl.ds(part * share + one, rows, stride=chi), :] = here[
                first : first + rows
            ]
        out.append(under(values).astype(BF16))

    def result():
        out_tails = [
            beside(
                [
                    side_out[(index * legs + leg) * chi : (index * legs + leg + 1) * chi, :]
                    for leg in range(legs)
                ]
            ).astype(BF16)
            for index in range(len(tails))
        ]
        return under(out), out_tails

    pieces = []
    for part in range(parts):
        pieces.append(functools.partial(start, part))
        pieces += [functools.partial(turn, part, half) for half in range(halves_of)]
    return pieces, result


def pass_site(main, tails, flat, matrix, sides):
    pieces, result = site_pieces(main, tails, flat, matrix, sides, 1)
    for piece in pieces:
        piece()
    return result()


def fold(end_main, end_tails, main, tails):
    total = mul_first(end_main, main)
    for end, tail in zip(end_tails, tails):
        total = total + mul_first(end, tail)
    return total


def spread(main, tails, end, tmp):
    chi = tails[0].shape[0]
    tmp[: chi * MAIN, :] = mul(main, end)
    parts = [tmp[pl.ds(leg, chi, stride=MAIN), :] for leg in range(MAIN)]
    return beside(parts + [mul(tail, end) for tail in tails])


def rescaled(value):
    return (value * lax.rsqrt(jnp.mean(value * value) + 1e-06)).astype(BF16)


def split(value):
    high = value.astype(BF16)
    return high, (value - high.astype(F32)).astype(BF16)


def mul_split(former, latter):
    (high, low), (other_high, other_low) = former, latter
    return mul(beside([high, low]), under([other_high, other_high])) + mul(high, other_low)


def inverse_roots(grams, pieces=()):
    pieces = list(pieces)
    step = lambda: pieces.pop(0)() if pieces else None
    chi = grams[0].shape[0]
    rows = lax.broadcasted_iota(jnp.int32, (chi, chi), 0)
    columns = lax.broadcasted_iota(jnp.int32, (chi, chi), 1)
    identity = jnp.where(rows == columns, 1.0, 0.0).astype(F32)
    scalings = [jnp.sum(gram * identity) + 1e-06 for gram in grams]
    currents = [gram / scaling for gram, scaling in zip(grams, scalings)]
    inverses = [1.5 * identity - 0.5 * current for current in currents]
    currents = [
        mul_split(split(current), split(inverse))
        for current, inverse in zip(currents, inverses)
    ]
    step()
    for iteration in range(1, NS_STEPS):
        nows = [split(current) for current in currents]
        invs = [split(inverse) for inverse in inverses]
        factors = [
            split(1.5 * identity - 0.5 * mul_split(inv, now)) for inv, now in zip(invs, nows)
        ]
        step()
        if iteration < NS_STEPS - 1:
            boths = [
                mul_split(factor, (beside([now[0], inv[0]]), beside([now[1], inv[1]])))
                for factor, now, inv in zip(factors, nows, invs)
            ]
            currents = [both[:, :chi] for both in boths]
            inverses = [both[:, chi:] for both in boths]
        else:
            inverses = [mul_split(factor, inv) for factor, inv in zip(factors, invs)]
        step()
    while pieces:
        step()
    return [
        beside(split(inverse * lax.rsqrt(scaling)))
        for inverse, scaling in zip(inverses, scalings)
    ]


def site_picks(bond, legs, size):
    shape = (size, bond**4)
    row = lax.broadcasted_iota(jnp.int32, shape, 0)
    column = lax.broadcasted_iota(jnp.int32, shape, 1)
    digit = lambda value, place: lax.rem(lax.div(value, bond**place), bond)
    late = row - legs * MAIN
    first = jnp.where(late < 0, lax.div(row, MAIN), lax.rem(jnp.maximum(late, 0), legs))
    second = jnp.where(
        late < 0, lax.rem(row, MAIN), MAIN + lax.div(jnp.maximum(late, 0), legs)
    )
    up, left, down, right = (digit(column, place) for place in (3, 2, 1, 0))
    picks = []
    for one, two in ((down, left), (right, up)):
        for place in (1, 0):
            hit = (digit(first, place) == one) & (digit(second, place) == two)
            picks.append(jnp.where(hit & (row < legs * legs), 1.0, 0.0).astype(F32))
    return picks


def site_kernel(ket_ref, forth_ref, back_ref, *, bond, legs):
    picks = site_picks(bond, legs, forth_ref.shape[0])
    forth = 0.0
    back = 0.0
    for phys in range(ket_ref.shape[0]):
        row = ket_ref[pl.ds(phys, 1), :]
        factors = []
        for first, second in ((0, 2), (2, 0)):
            for layer in range(2):
                factors.append(
                    lax.dot_general(
                        picks[first + layer] * row, picks[second + layer],
                        (((1,), (1,)), ((), ())), precision=HIGHEST, preferred_element_type=F32,
                    )
                )
        forth = forth + factors[0] * factors[1]
        back = back + factors[2] * factors[3]
    forth_ref[...] = forth.astype(BF16)
    back_ref[...] = back.astype(BF16)


def lower_kernel(
    corner_ref, bottom_ref, left_ref, sketch_ref, back_ref,
    lower_ref, pair_ref, left_main_ref, tmp, side,
):
    legs = left_ref.shape[0]
    left = legs_of_first(left_ref)
    left_main_ref[...] = main_of_legs(left, tmp)
    pair = mul(corner_ref[...], beside(legs_of_first(bottom_ref))).astype(BF16)
    pair_ref[...] = pair
    folded = under(legs_of_rows(sketch_ref[1], tmp, legs))
    passed, tails = pass_site(left_main_ref[...], left[MAIN:], pair, back_ref[...], side)
    lower_ref[...] = spread(passed, tails, folded, tmp).astype(BF16)


def right_kernel(
    corner_ref, edge_ref, top_ref, sketch_ref, forth_ref,
    upper_ref, lower_next_ref, bottom_pair_ref, inverse_ref,
    right_ref, pair_ref, top_main_ref, left_sketch_ref, bottom_ref, tmp, side,
):
    chi = upper_ref.shape[0]
    cut = under(cut_legs(upper_ref, lower_next_ref))
    corner = mul_first(cut, under(legs_of_flat(bottom_pair_ref[...], chi))).astype(BF16)
    bottom_ref[...] = rescaled(left_times(inverse_ref[...], corner))
    legs = edge_ref.shape[0]
    top = legs_of_first(top_ref)
    top_main_ref[...] = main_of_legs(top, tmp)
    pair = mul(corner_ref[...], beside(legs_of_first(edge_ref))).astype(BF16)
    pair_ref[...] = pair
    left_sketch_ref[...] = beside(legs_of_rows(sketch_ref[0], tmp, legs))
    folded = under(legs_of_rows(sketch_ref[1], tmp, legs))
    passed, tails = pass_site(top_main_ref[...], top[MAIN:], pair, forth_ref[...], side)
    right_ref[...] = spread(passed, tails, folded, tmp).astype(BF16)


def upper_kernel(
    corner_ref, top_ref, left_main_ref, left_ref, sketch_ref, forth_ref,
    upper_ref, pair_ref, tmp, side,
):
    legs, chi, _ = left_ref.shape
    pair = mul_first(corner_ref[...], beside(legs_of_first(top_ref))).astype(BF16)
    pair_ref[...] = pair
    parts = legs_of_flat(pair, chi)
    sketch = beside(legs_of_rows(sketch_ref[0], tmp, legs))
    main = main_of_legs(parts, tmp)
    passed, tails = pass_site(main, parts[MAIN:], sketch, forth_ref[...], side)
    ends = legs_of_first(left_ref)[MAIN:]
    upper_ref[...] = fold(left_main_ref[...], ends, passed, tails).astype(BF16)


def cut_legs(former_ref, latter_ref):
    chi = former_ref.shape[0]
    cut = former_ref[...].astype(F32) + latter_ref[...].astype(F32)
    return legs_of_flat(cut.astype(BF16), chi)


def halves(value):
    chi = value.shape[1] // 2
    return value[:, :chi] + value[:, chi:]


def right_times(value, inverse):
    return halves(mul(value, inverse))


def left_times(inverse, value):
    chi = inverse.shape[0]
    both = mul_first(inverse, value)
    return both[:chi] + both[chi:]


def pass_kernel(
    former_ref, latter_ref, main_ref, edge_ref, matrix_ref, passed_ref, tails_ref, side
):
    cut = cut_legs(former_ref, latter_ref)
    passed, tails = pass_site(
        main_ref[...], legs_of_first(edge_ref)[MAIN:], beside(cut), matrix_ref[...], side
    )
    passed_ref[...] = passed
    for index, tail in enumerate(tails):
        tails_ref[index] = tail


def up_pass_kernel(
    former_ref, latter_ref, main_ref, edge_ref, matrix_ref, pair_ref,
    inverse_ref, corner_ref, passed_ref, tails_ref, side,
):
    cut = cut_legs(former_ref, latter_ref)
    rows = under(cut)
    pieces, result = site_pieces(
        main_ref[...], legs_of_first(edge_ref)[MAIN:], beside(cut), matrix_ref[...], side, 4
    )
    corner = []

    def corner_piece():
        pair = under(legs_of_flat(pair_ref[...], former_ref.shape[0]))
        corner.append(mul_first(rows, pair).astype(BF16))

    (inverse,) = inverse_roots([mul_first(rows, rows)], [corner_piece] + pieces)
    inverse_ref[...] = inverse
    corner_ref[...] = rescaled(left_times(inverse, corner[0]))
    passed, tails = result()
    passed_ref[...] = passed
    for index, tail in enumerate(tails):
        tails_ref[index] = tail


def folded_cut(cut, passed_ref, tails_ref, tmp):
    tails = [tails_ref[index] for index in range(tails_ref.shape[0])]
    return fold(main_of_legs(cut, tmp), cut[MAIN:], passed_ref[...], tails).astype(BF16)


def left_move_kernel(
    upper_ref, lower_next_ref, upper_before_ref, lower_ref, top_pair_ref,
    passed_ref, tails_ref, moved_ref, inverse_ref, tmp,
):
    chi = upper_ref.shape[0]
    below = cut_legs(upper_ref, lower_next_ref)
    above = cut_legs(upper_before_ref, lower_ref)
    rows_below, rows_above = under(below), under(above)
    grams = [mul_first(rows_below, rows_below), mul_first(rows_above, rows_above)]
    corners = []
    edge = []
    main = main_of_legs(above, tmp).T
    tails = [(end.T, tails_ref[index]) for index, end in enumerate(above[MAIN:])]

    def top_piece():
        pair = under(legs_of_flat(top_pair_ref[...], chi))
        corners.append(mul_first(pair, rows_above).astype(BF16))

    def edge_piece(start):
        here = slice(start, start + chi)
        part = mul(main, passed_ref[:, here])
        for end, tail in tails:
            part = part + mul(end, tail[:, here])
        edge.append(part.astype(BF16))

    pieces = [top_piece]
    pieces += [functools.partial(edge_piece, at) for at in range(0, passed_ref.shape[1], chi)]
    inverse_below, inverse_above = inverse_roots(grams, pieces)
    inverse_ref[...] = inverse_below
    edge = beside(edge)
    turned = left_times(inverse_above, edge).astype(BF16)
    rows = rescaled(right_times(under(legs_of_flat(turned, chi)), inverse_below))
    moved_ref[...] = beside(
        [rows[start : start + chi] for start in range(0, rows.shape[0], chi)]
        + [rescaled(right_times(corners[0], inverse_above))]
    )


def left_cut_kernel(
    moved_ref, top_main_ref, top_ref, back_ref, sketch_ref,
    edge_ref, term_ref, pair_ref, tmp, side, sems,
):
    legs, chi, _ = top_ref.shape
    part = lambda leg: moved_ref.at[:, leg * chi : (leg + 1) * chi]
    outs = [edge_ref.at[leg] for leg in range(legs)]
    stores = [pltpu.make_async_copy(part(leg), outs[leg], sems.at[leg]) for leg in range(legs)]
    for store in stores:
        store.start()
    corner = moved_ref[:, legs * chi : (legs + 1) * chi]
    pair = mul(corner, moved_ref[:, : legs * chi]).astype(BF16)
    pair_ref[...] = pair
    parts = legs_of_flat(pair, chi)
    main = main_of_legs(parts, tmp)
    passed, tails = pass_site(main, parts[MAIN:], sketch_ref[...], back_ref[...], side)
    ends = legs_of_first(top_ref)[MAIN:]
    term_ref[...] = fold(top_main_ref[...], ends, passed, tails).astype(BF16)
    for store in stores:
        store.wait()


def up_move_kernel(
    term_before_ref, right_ref, left_pair_ref, passed_ref, tails_ref, inverse_ref, corner_ref,
    moved_ref, tmp,
):
    chi = right_ref.shape[0]
    west = cut_legs(term_before_ref, right_ref)
    left = mul_first(under(west), under(legs_of_flat(left_pair_ref[...], chi)))
    edge = under(legs_of_flat(folded_cut(west, passed_ref, tails_ref, tmp), chi))
    rows = right_times(edge, inverse_ref[...]).astype(BF16)
    moved_ref[...] = beside(
        [rows[start : start + chi] for start in range(0, rows.shape[0], chi)]
        + [left.astype(BF16), corner_ref[...]]
    )


def finish_kernel(
    moved_ref, west_ref, bottom_ref, edge_ref, left_ref, right_ref, bottom_out_ref,
    edge, left, sems,
):
    legs, chi, _ = edge.shape
    right_part = moved_ref.at[:, (legs + 1) * chi :]
    stores = [
        pltpu.make_async_copy(right_part, right_ref, sems.at[0]),
        pltpu.make_async_copy(bottom_ref, bottom_out_ref, sems.at[3]),
    ]
    for store in stores:
        store.start()
    both = left_times(west_ref[...], moved_ref[:, : (legs + 1) * chi])
    left[...] = rescaled(both[:, legs * chi :])
    stores.append(pltpu.make_async_copy(left, left_ref, sems.at[1]))
    stores[-1].start()
    flat = rescaled(both[:, : legs * chi])
    for leg, part in enumerate(legs_of_flat(flat, chi)):
        edge[leg] = part
    stores.append(pltpu.make_async_copy(edge, edge_ref, sems.at[2]))
    stores[-1].start()
    for store in stores:
        store.wait()


def kernel_call(kernel, micros, outs, scratch, *operands, stores=0):
    place = lambda own: pl.BlockSpec(memory_space=pltpu.HBM if own else pltpu.VMEM)
    return pl.pallas_call(
        kernel,
        out_shape=[jax.ShapeDtypeStruct(shape, BF16) for shape in outs],
        in_specs=[place(False)] * len(operands),
        out_specs=[place(index < stores) for index in range(len(outs))],
        scratch_shapes=scratch,
        compiler_params=pltpu.CompilerParams(vmem_limit_bytes=40 * 2**20),
        cost_estimate=pl.CostEstimate(
            flops=int(micros * 1e9), bytes_accessed=0, transcendentals=0
        ),
    )(*operands)


def local(
    ket, corner_tl, corner_tr, corner_bl, edge_left, edge_top, edge_right, edge_bottom,
    row_sketch, col_sketch,
):
    squeeze = lambda value: value.reshape(value.shape[2:])
    legs_first = lambda value: jnp.swapaxes(squeeze(value), 0, 1)
    ket, corner_tl, corner_tr, corner_bl = map(squeeze, (ket, corner_tl, corner_tr, corner_bl))
    edge_left, edge_top, edge_right, edge_bottom = map(
        legs_first, (edge_left, edge_top, edge_right, edge_bottom)
    )
    row_sketch, col_sketch = map(squeeze, (row_sketch, col_sketch))
    legs, chi, _ = edge_left.shape
    bond = round(legs**0.5)
    size = padded(legs * legs, 32)
    flat = (chi, legs * chi)
    main = (chi * MAIN, chi)
    square = (chi, chi)
    pair_of = (chi, 2 * chi)
    site = (size, size)
    moved_one = (chi, (legs + 1) * chi)
    moved_two = (chi, (legs + 2) * chi)
    passed_main = (chi * MAIN, legs * chi)
    passed_tails = (legs - MAIN, chi, legs * chi)
    tmp = pltpu.VMEM((chi * legs, chi), F32)
    side = pltpu.VMEM((2, padded((legs - MAIN) * legs, MAIN) * chi, chi), F32)
    short = lambda value: pltpu.VMEM(value, BF16)

    forth, back = kernel_call(
        functools.partial(site_kernel, bond=bond, legs=legs), 10, [site, site], [], ket
    )
    lower, bottom_pair, left_main = kernel_call(
        lower_kernel, 20, [flat, flat, main], [tmp, side],
        corner_bl, edge_bottom, edge_left, row_sketch, back,
    )
    lower_next = lax.ppermute(lower, "row", ring("row", -1))
    upper, top_pair = kernel_call(
        upper_kernel, 20, [flat, flat], [tmp, side],
        corner_tl, edge_top, left_main, edge_left, row_sketch, forth,
    )
    upper_before = lax.ppermute(upper, "row", ring("row", 1))
    passed, tails = kernel_call(
        pass_kernel, 0.02, [passed_main, passed_tails], [side],
        upper, lower_next, left_main, edge_left, back,
    )
    moved_left, inverse = kernel_call(
        left_move_kernel, 0.02, [moved_one, pair_of], [tmp],
        upper, lower_next, upper_before, lower, top_pair, passed, tails,
    )
    moved_left, inverse = lax.optimization_barrier((moved_left, inverse))
    moved_left = lax.ppermute(moved_left, "col", ring("col", 1))
    right, right_pair, top_main, left_sketch, bottom_mid = kernel_call(
        right_kernel, 20, [flat, flat, main, flat, square], [tmp, side],
        corner_tr, edge_right, edge_top, col_sketch, forth,
        upper, lower_next, bottom_pair, inverse,
    )
    right_next = lax.ppermute(right, "col", ring("col", -1))
    corner_bl_new = lax.ppermute(bottom_mid, "col", ring("col", 1))
    edge_left_new, term, left_pair = kernel_call(
        left_cut_kernel, 0.02, [edge_left.shape, flat, flat],
        [tmp, side, pltpu.SemaphoreType.DMA((legs,))],
        moved_left, top_main, edge_top, back, left_sketch, stores=1,
    )
    term_before = lax.ppermute(term, "col", ring("col", 1))
    inverse, right_up, passed, tails = kernel_call(
        up_pass_kernel, 0.02, [pair_of, square, passed_main, passed_tails], [side],
        term, right_next, top_main, edge_top, forth, right_pair,
    )
    west = lax.ppermute(inverse, ("row", "col"), diagonal())
    term_before, passed, corner_bl_new = lax.optimization_barrier(
        (term_before, passed, corner_bl_new)
    )
    (moved_up,) = kernel_call(
        up_move_kernel, 0.02, [moved_two], [tmp],
        term_before, right, left_pair, passed, tails, inverse, right_up,
    )
    moved_up = lax.ppermute(moved_up, "row", ring("row", 1))
    edge_top_new, corner_tl_new, corner_tr_new, corner_bl_new = kernel_call(
        finish_kernel, 0.02, [edge_top.shape, square, square, square],
        [short(edge_top.shape), short(square), pltpu.SemaphoreType.DMA((4,))],
        moved_up, west, corner_bl_new, stores=4,
    )
    outs = (
        jnp.swapaxes(edge_left_new, 0, 1), corner_bl_new,
        jnp.swapaxes(edge_top_new, 0, 1), corner_tl_new, corner_tr_new,
    )
    return tuple(value.reshape((1, 1) + value.shape) for value in outs)


def solution(mesh):
    matrix = P("row", "col", None, None)
    tensor = P("row", "col", None, None, None)
    return jax.shard_map(
        local,
        mesh=mesh,
        in_specs=(matrix,) * 4 + (tensor,) * 6,
        out_specs=(tensor, matrix, tensor, matrix, matrix),
        check_vma=False,
    )
```

```python
import functools

import jax
import jax.numpy as jnp
from jax import lax
from jax.experimental import pallas as pl
from jax.experimental.pallas import tpu as pltpu
from jax.sharding import PartitionSpec as P

NS_STEPS = 8
MAIN = 8
F32 = jnp.float32
BF16 = jnp.bfloat16
HIGHEST = lax.Precision.HIGHEST


def ring(axis, steps):
    count = lax.axis_size(axis)
    return [(source, (source + steps) % count) for source in range(count)]


def diagonal():
    rows, cols = lax.axis_size("row"), lax.axis_size("col")
    return [
        (row * cols + col, (row + 1) % rows * cols + (col + 1) % cols)
        for row in range(rows)
        for col in range(cols)
    ]


def padded(count, multiple):
    return -(-count // multiple) * multiple


def mul(former, latter):
    return jnp.dot(former, latter, preferred_element_type=F32)


def mul_first(former, latter):
    return lax.dot_general(former, latter, (((0,), (0,)), ((), ())), preferred_element_type=F32)


def beside(parts):
    return jnp.concatenate(parts, axis=1)


def under(parts):
    return jnp.concatenate(parts, axis=0)


def legs_of_flat(flat, chi):
    return [flat[:, start : start + chi] for start in range(0, flat.shape[1], chi)]


def legs_of_first(ref):
    return [ref[leg] for leg in range(ref.shape[0])]


def legs_of_rows(rows, tmp, legs):
    count = rows.shape[0]
    tmp[:count, :] = rows.astype(F32)
    return [
        tmp[pl.ds(leg, count // legs, stride=legs), :].astype(BF16) for leg in range(legs)
    ]


def main_of_legs(parts, tmp):
    chi = parts[0].shape[0]
    for leg in range(MAIN):
        tmp[pl.ds(leg, chi, stride=MAIN), :] = parts[leg].astype(F32)
    return tmp[: chi * MAIN, :].astype(BF16)


def site_pieces(main, tails, flat, matrix, sides, parts):
    chi = tails[0].shape[0]
    legs = flat.shape[1] // chi
    size = matrix.shape[0]
    first = legs * MAIN
    used = len(tails) * legs
    rows = padded(used, MAIN)
    side, side_out = sides.at[0], sides.at[1]
    fill = [jnp.zeros((size - first - rows, chi), F32)] if size > first + rows else []
    blocks, out = [], []
    share = chi // parts
    halves_of = 2 if parts > 1 else 1

    def start(part):
        here = main[part * share * MAIN : (part + 1) * share * MAIN]
        if part:
            blocks.append(mul(here, flat))
            return
        block = mul(under(tails + [here]), flat)
        for index in range(len(tails)):
            tail = block[index * chi : (index + 1) * chi]
            for leg, value in enumerate(legs_of_flat(tail, chi)):
                at = (index * legs + leg) * chi
                side[at : at + chi, :] = value
        side[used * chi : rows * chi, :] = jnp.zeros(((rows - used) * chi, chi), F32)
        blocks.append(block[len(tails) * chi :])

    def turn(part, half):
        count = share // halves_of
        ones = [half * count + one for one in range(count)]
        columns = beside(
            [
                under(
                    legs_of_flat(blocks[part][one * MAIN : (one + 1) * MAIN, :], chi)
                    + [side[pl.ds(part * share + one, rows, stride=chi), :]]
                    + fill
                ).astype(BF16)
                for one in ones
            ]
        )
        passed = mul(matrix, columns)
        values = []
        for at, one in enumerate(ones):
            here = passed[:, at * chi : (at + 1) * chi]
            values.append(beside([here[leg * MAIN : (leg + 1) * MAIN] for leg in range(legs)]))
            side_out[pl.ds(part * share + one, rows, stride=chi), :] = here[
                first : first + rows
            ]
        out.append(under(values).astype(BF16))

    def result():
        out_tails = [
            beside(
                [
                    side_out[(index * legs + leg) * chi : (index * legs + leg + 1) * chi, :]
                    for leg in range(legs)
                ]
            ).astype(BF16)
            for index in range(len(tails))
        ]
        return under(out), out_tails

    pieces = []
    for part in range(parts):
        pieces.append(functools.partial(start, part))
        pieces += [functools.partial(turn, part, half) for half in range(halves_of)]
    return pieces, result


def pass_site(main, tails, flat, matrix, sides):
    pieces, result = site_pieces(main, tails, flat, matrix, sides, 1)
    for piece in pieces:
        piece()
    return result()


def fold(end_main, end_tails, main, tails):
    return mul_first(under([end_main] + end_tails), under([main] + tails))


def spread(main, tails, end, tmp):
    chi = tails[0].shape[0]
    tmp[: chi * MAIN, :] = mul(main, end)
    parts = [tmp[pl.ds(leg, chi, stride=MAIN), :] for leg in range(MAIN)]
    return beside(parts + [mul(tail, end) for tail in tails])


def rescaled(value):
    return (value * lax.rsqrt(jnp.mean(value * value) + 1e-06)).astype(BF16)


def split(value):
    high = value.astype(BF16)
    return high, (value - high.astype(F32)).astype(BF16)


def mul_split(former, latter):
    (high, low), (other_high, other_low) = former, latter
    return mul(beside([high, low]), under([other_high, other_high])) + mul(high, other_low)


def inverse_roots(grams, pieces=()):
    pieces = list(pieces)
    step = lambda: pieces.pop(0)() if pieces else None
    chi = grams[0].shape[0]
    rows = lax.broadcasted_iota(jnp.int32, (chi, chi), 0)
    columns = lax.broadcasted_iota(jnp.int32, (chi, chi), 1)
    identity = jnp.where(rows == columns, 1.0, 0.0).astype(F32)
    scalings = [jnp.sum(gram * identity) + 1e-06 for gram in grams]
    currents = [gram / scaling for gram, scaling in zip(grams, scalings)]
    inverses = [1.5 * identity - 0.5 * current for current in currents]
    currents = [
        mul_split(split(current), split(inverse))
        for current, inverse in zip(currents, inverses)
    ]
    step()
    for iteration in range(1, NS_STEPS):
        nows = [split(current) for current in currents]
        invs = [split(inverse) for inverse in inverses]
        factors = [
            split(1.5 * identity - 0.5 * mul_split(inv, now)) for inv, now in zip(invs, nows)
        ]
        step()
        if iteration < NS_STEPS - 1:
            boths = [
                mul_split(factor, (beside([now[0], inv[0]]), beside([now[1], inv[1]])))
                for factor, now, inv in zip(factors, nows, invs)
            ]
            currents = [both[:, :chi] for both in boths]
            inverses = [both[:, chi:] for both in boths]
        else:
            inverses = [mul_split(factor, inv) for factor, inv in zip(factors, invs)]
        step()
    while pieces:
        step()
    return [
        beside(split(inverse * lax.rsqrt(scaling)))
        for inverse, scaling in zip(inverses, scalings)
    ]


def site_picks(bond, legs, size):
    shape = (size, bond**4)
    row = lax.broadcasted_iota(jnp.int32, shape, 0)
    column = lax.broadcasted_iota(jnp.int32, shape, 1)
    digit = lambda value, place: lax.rem(lax.div(value, bond**place), bond)
    late = row - legs * MAIN
    first = jnp.where(late < 0, lax.div(row, MAIN), lax.rem(jnp.maximum(late, 0), legs))
    second = jnp.where(
        late < 0, lax.rem(row, MAIN), MAIN + lax.div(jnp.maximum(late, 0), legs)
    )
    up, left, down, right = (digit(column, place) for place in (3, 2, 1, 0))
    picks = []
    for one, two in ((down, left), (right, up)):
        for place in (1, 0):
            hit = (digit(first, place) == one) & (digit(second, place) == two)
            picks.append(jnp.where(hit & (row < legs * legs), 1.0, 0.0).astype(F32))
    return picks


def site_kernel(ket_ref, forth_ref, back_ref, *, bond, legs):
    picks = site_picks(bond, legs, forth_ref.shape[0])
    forth = 0.0
    back = 0.0
    for phys in range(ket_ref.shape[0]):
        row = ket_ref[pl.ds(phys, 1), :]
        factors = []
        for first, second in ((0, 2), (2, 0)):
            for layer in range(2):
                factors.append(
                    lax.dot_general(
                        picks[first + layer] * row, picks[second + layer],
                        (((1,), (1,)), ((), ())), precision=HIGHEST, preferred_element_type=F32,
                    )
                )
        forth = forth + factors[0] * factors[1]
        back = back + factors[2] * factors[3]
    forth_ref[...] = forth.astype(BF16)
    back_ref[...] = back.astype(BF16)


def lower_kernel(
    corner_ref, bottom_ref, left_ref, sketch_ref, back_ref,
    lower_ref, pair_ref, left_main_ref, tmp, side,
):
    legs = left_ref.shape[0]
    left = legs_of_first(left_ref)
    left_main_ref[...] = main_of_legs(left, tmp)
    pair = mul(corner_ref[...], beside(legs_of_first(bottom_ref))).astype(BF16)
    pair_ref[...] = pair
    folded = under(legs_of_rows(sketch_ref[1], tmp, legs))
    passed, tails = pass_site(left_main_ref[...], left[MAIN:], pair, back_ref[...], side)
    lower_ref[...] = spread(passed, tails, folded, tmp).astype(BF16)


def right_kernel(
    corner_ref, edge_ref, top_ref, sketch_ref, forth_ref,
    upper_ref, lower_next_ref, bottom_pair_ref, inverse_ref,
    right_ref, pair_ref, top_main_ref, left_sketch_ref, bottom_ref, tmp, side,
):
    chi = upper_ref.shape[0]
    cut = under(cut_legs(upper_ref, lower_next_ref))
    corner = mul_first(cut, under(legs_of_flat(bottom_pair_ref[...], chi))).astype(BF16)
    bottom_ref[...] = rescaled(left_times(inverse_ref[...], corner))
    legs = edge_ref.shape[0]
    top = legs_of_first(top_ref)
    top_main_ref[...] = main_of_legs(top, tmp)
    pair = mul(corner_ref[...], beside(legs_of_first(edge_ref))).astype(BF16)
    pair_ref[...] = pair
    left_sketch_ref[...] = beside(legs_of_rows(sketch_ref[0], tmp, legs))
    folded = under(legs_of_rows(sketch_ref[1], tmp, legs))
    passed, tails = pass_site(top_main_ref[...], top[MAIN:], pair, forth_ref[...], side)
    right_ref[...] = spread(passed, tails, folded, tmp).astype(BF16)


def upper_kernel(
    corner_ref, top_ref, left_main_ref, left_ref, sketch_ref, forth_ref,
    upper_ref, pair_ref, tmp, side,
):
    legs, chi, _ = left_ref.shape
    pair = mul_first(corner_ref[...], beside(legs_of_first(top_ref))).astype(BF16)
    pair_ref[...] = pair
    parts = legs_of_flat(pair, chi)
    sketch = beside(legs_of_rows(sketch_ref[0], tmp, legs))
    main = main_of_legs(parts, tmp)
    passed, tails = pass_site(main, parts[MAIN:], sketch, forth_ref[...], side)
    ends = legs_of_first(left_ref)[MAIN:]
    upper_ref[...] = fold(left_main_ref[...], ends, passed, tails).astype(BF16)


def cut_legs(former_ref, latter_ref):
    chi = former_ref.shape[0]
    cut = former_ref[...].astype(F32) + latter_ref[...].astype(F32)
    return legs_of_flat(cut.astype(BF16), chi)


def halves(value):
    chi = value.shape[1] // 2
    return value[:, :chi] + value[:, chi:]


def right_times(value, inverse):
    return halves(mul(value, inverse))


def left_times(inverse, value):
    chi = inverse.shape[0]
    both = mul_first(inverse, value)
    return both[:chi] + both[chi:]


def pass_kernel(
    former_ref, latter_ref, main_ref, edge_ref, matrix_ref, passed_ref, tails_ref, side
):
    cut = cut_legs(former_ref, latter_ref)
    passed, tails = pass_site(
        main_ref[...], legs_of_first(edge_ref)[MAIN:], beside(cut), matrix_ref[...], side
    )
    passed_ref[...] = passed
    for index, tail in enumerate(tails):
        tails_ref[index] = tail


def up_pass_kernel(
    former_ref, latter_ref, main_ref, edge_ref, matrix_ref, pair_ref,
    inverse_ref, corner_ref, passed_ref, tails_ref, side,
):
    cut = cut_legs(former_ref, latter_ref)
    rows = under(cut)
    pieces, result = site_pieces(
        main_ref[...], legs_of_first(edge_ref)[MAIN:], beside(cut), matrix_ref[...], side, 4
    )
    corner = []

    def corner_piece():
        pair = under(legs_of_flat(pair_ref[...], former_ref.shape[0]))
        corner.append(mul_first(rows, pair).astype(BF16))

    (inverse,) = inverse_roots([mul_first(rows, rows)], [corner_piece] + pieces)
    inverse_ref[...] = inverse
    corner_ref[...] = rescaled(left_times(inverse, corner[0]))
    passed, tails = result()
    passed_ref[...] = passed
    for index, tail in enumerate(tails):
        tails_ref[index] = tail


def folded_cut(cut, passed_ref, tails_ref, tmp):
    tails = [tails_ref[index] for index in range(tails_ref.shape[0])]
    return fold(main_of_legs(cut, tmp), cut[MAIN:], passed_ref[...], tails).astype(BF16)


def left_move_kernel(
    upper_ref, lower_next_ref, upper_before_ref, lower_ref, top_pair_ref,
    passed_ref, tails_ref, moved_ref, inverse_ref, tmp,
):
    chi = upper_ref.shape[0]
    below = cut_legs(upper_ref, lower_next_ref)
    above = cut_legs(upper_before_ref, lower_ref)
    rows_below, rows_above = under(below), under(above)
    grams = [mul_first(rows_below, rows_below), mul_first(rows_above, rows_above)]
    corners = []
    edge = []
    main = main_of_legs(above, tmp).T
    tails = [(end.T, tails_ref[index]) for index, end in enumerate(above[MAIN:])]

    def top_piece():
        pair = under(legs_of_flat(top_pair_ref[...], chi))
        corners.append(mul_first(pair, rows_above).astype(BF16))

    def edge_piece(start):
        here = slice(start, start + chi)
        part = mul(main, passed_ref[:, here])
        for end, tail in tails:
            part = part + mul(end, tail[:, here])
        edge.append(part.astype(BF16))

    pieces = [top_piece]
    pieces += [functools.partial(edge_piece, at) for at in range(0, passed_ref.shape[1], chi)]
    inverse_below, inverse_above = inverse_roots(grams, pieces)
    inverse_ref[...] = inverse_below
    edge = beside(edge)
    turned = left_times(inverse_above, edge).astype(BF16)
    rows = rescaled(right_times(under(legs_of_flat(turned, chi)), inverse_below))
    moved_ref[...] = beside(
        [rows[start : start + chi] for start in range(0, rows.shape[0], chi)]
        + [rescaled(right_times(corners[0], inverse_above))]
    )


def left_cut_kernel(
    moved_ref, top_main_ref, top_ref, back_ref, sketch_ref,
    edge_ref, term_ref, pair_ref, tmp, side, sems,
):
    legs, chi, _ = top_ref.shape
    part = lambda leg: moved_ref.at[:, leg * chi : (leg + 1) * chi]
    outs = [edge_ref.at[leg] for leg in range(legs)]
    stores = [pltpu.make_async_copy(part(leg), outs[leg], sems.at[leg]) for leg in range(legs)]
    for store in stores:
        store.start()
    corner = moved_ref[:, legs * chi : (legs + 1) * chi]
    pair = mul(corner, moved_ref[:, : legs * chi]).astype(BF16)
    pair_ref[...] = pair
    parts = legs_of_flat(pair, chi)
    main = main_of_legs(parts, tmp)
    passed, tails = pass_site(main, parts[MAIN:], sketch_ref[...], back_ref[...], side)
    ends = legs_of_first(top_ref)[MAIN:]
    term_ref[...] = fold(top_main_ref[...], ends, passed, tails).astype(BF16)
    for store in stores:
        store.wait()


def up_move_kernel(
    term_before_ref, right_ref, left_pair_ref, passed_ref, tails_ref, inverse_ref, corner_ref,
    moved_ref, tmp,
):
    chi = right_ref.shape[0]
    west = cut_legs(term_before_ref, right_ref)
    left = mul_first(under(west), under(legs_of_flat(left_pair_ref[...], chi)))
    edge = under(legs_of_flat(folded_cut(west, passed_ref, tails_ref, tmp), chi))
    rows = right_times(edge, inverse_ref[...]).astype(BF16)
    moved_ref[...] = beside(
        [rows[start : start + chi] for start in range(0, rows.shape[0], chi)]
        + [left.astype(BF16), corner_ref[...]]
    )


def finish_kernel(
    moved_ref, west_ref, bottom_ref, edge_ref, left_ref, right_ref, bottom_out_ref,
    edge, left, sems,
):
    legs, chi, _ = edge.shape
    right_part = moved_ref.at[:, (legs + 1) * chi :]
    stores = [
        pltpu.make_async_copy(right_part, right_ref, sems.at[0]),
        pltpu.make_async_copy(bottom_ref, bottom_out_ref, sems.at[3]),
    ]
    for store in stores:
        store.start()
    both = left_times(west_ref[...], moved_ref[:, : (legs + 1) * chi])
    left[...] = rescaled(both[:, legs * chi :])
    stores.append(pltpu.make_async_copy(left, left_ref, sems.at[1]))
    stores[-1].start()
    flat = rescaled(both[:, : legs * chi])
    for leg, part in enumerate(legs_of_flat(flat, chi)):
        edge[leg] = part
    stores.append(pltpu.make_async_copy(edge, edge_ref, sems.at[2]))
    stores[-1].start()
    for store in stores:
        store.wait()


def kernel_call(kernel, micros, outs, scratch, *operands, stores=0):
    place = lambda own: pl.BlockSpec(memory_space=pltpu.HBM if own else pltpu.VMEM)
    return pl.pallas_call(
        kernel,
        out_shape=[jax.ShapeDtypeStruct(shape, BF16) for shape in outs],
        in_specs=[place(False)] * len(operands),
        out_specs=[place(index < stores) for index in range(len(outs))],
        scratch_shapes=scratch,
        compiler_params=pltpu.CompilerParams(vmem_limit_bytes=40 * 2**20),
        cost_estimate=pl.CostEstimate(
            flops=int(micros * 1e9), bytes_accessed=0, transcendentals=0
        ),
    )(*operands)


def local(
    ket, corner_tl, corner_tr, corner_bl, edge_left, edge_top, edge_right, edge_bottom,
    row_sketch, col_sketch,
):
    squeeze = lambda value: value.reshape(value.shape[2:])
    legs_first = lambda value: jnp.swapaxes(squeeze(value), 0, 1)
    ket, corner_tl, corner_tr, corner_bl = map(squeeze, (ket, corner_tl, corner_tr, corner_bl))
    edge_left, edge_top, edge_right, edge_bottom = map(
        legs_first, (edge_left, edge_top, edge_right, edge_bottom)
    )
    row_sketch, col_sketch = map(squeeze, (row_sketch, col_sketch))
    legs, chi, _ = edge_left.shape
    bond = round(legs**0.5)
    size = padded(legs * legs, 32)
    flat = (chi, legs * chi)
    main = (chi * MAIN, chi)
    square = (chi, chi)
    pair_of = (chi, 2 * chi)
    site = (size, size)
    moved_one = (chi, (legs + 1) * chi)
    moved_two = (chi, (legs + 2) * chi)
    passed_main = (chi * MAIN, legs * chi)
    passed_tails = (legs - MAIN, chi, legs * chi)
    tmp = pltpu.VMEM((chi * legs, chi), F32)
    side = pltpu.VMEM((2, padded((legs - MAIN) * legs, MAIN) * chi, chi), F32)
    short = lambda value: pltpu.VMEM(value, BF16)

    forth, back = kernel_call(
        functools.partial(site_kernel, bond=bond, legs=legs), 10, [site, site], [], ket
    )
    lower, bottom_pair, left_main = kernel_call(
        lower_kernel, 20, [flat, flat, main], [tmp, side],
        corner_bl, edge_bottom, edge_left, row_sketch, back,
    )
    lower_next = lax.ppermute(lower, "row", ring("row", -1))
    upper, top_pair = kernel_call(
        upper_kernel, 20, [flat, flat], [tmp, side],
        corner_tl, edge_top, left_main, edge_left, row_sketch, forth,
    )
    upper_before = lax.ppermute(upper, "row", ring("row", 1))
    passed, tails = kernel_call(
        pass_kernel, 0.02, [passed_main, passed_tails], [side],
        upper, lower_next, left_main, edge_left, back,
    )
    moved_left, inverse = kernel_call(
        left_move_kernel, 0.02, [moved_one, pair_of], [tmp],
        upper, lower_next, upper_before, lower, top_pair, passed, tails,
    )
    moved_left, inverse = lax.optimization_barrier((moved_left, inverse))
    moved_left = lax.ppermute(moved_left, "col", ring("col", 1))
    right, right_pair, top_main, left_sketch, bottom_mid = kernel_call(
        right_kernel, 20, [flat, flat, main, flat, square], [tmp, side],
        corner_tr, edge_right, edge_top, col_sketch, forth,
        upper, lower_next, bottom_pair, inverse,
    )
    right_next = lax.ppermute(right, "col", ring("col", -1))
    corner_bl_new = lax.ppermute(bottom_mid, "col", ring("col", 1))
    edge_left_new, term, left_pair = kernel_call(
        left_cut_kernel, 0.02, [edge_left.shape, flat, flat],
        [tmp, side, pltpu.SemaphoreType.DMA((legs,))],
        moved_left, top_main, edge_top, back, left_sketch, stores=1,
    )
    term_before = lax.ppermute(term, "col", ring("col", 1))
    inverse, right_up, passed, tails = kernel_call(
        up_pass_kernel, 0.02, [pair_of, square, passed_main, passed_tails], [side],
        term, right_next, top_main, edge_top, forth, right_pair,
    )
    west = lax.ppermute(inverse, ("row", "col"), diagonal())
    term_before, passed, corner_bl_new = lax.optimization_barrier(
        (term_before, passed, corner_bl_new)
    )
    (moved_up,) = kernel_call(
        up_move_kernel, 0.02, [moved_two], [tmp],
        term_before, right, left_pair, passed, tails, inverse, right_up,
    )
    moved_up = lax.ppermute(moved_up, "row", ring("row", 1))
    edge_top_new, corner_tl_new, corner_tr_new, corner_bl_new = kernel_call(
        finish_kernel, 0.02, [edge_top.shape, square, square, square],
        [short(edge_top.shape), short(square), pltpu.SemaphoreType.DMA((4,))],
        moved_up, west, corner_bl_new, stores=4,
    )
    outs = (
        jnp.swapaxes(edge_left_new, 0, 1), corner_bl_new,
        jnp.swapaxes(edge_top_new, 0, 1), corner_tl_new, corner_tr_new,
    )
    return tuple(value.reshape((1, 1) + value.shape) for value in outs)


def solution(mesh):
    matrix = P("row", "col", None, None)
    tensor = P("row", "col", None, None, None)
    return jax.shard_map(
        local,
        mesh=mesh,
        in_specs=(matrix,) * 4 + (tensor,) * 6,
        out_specs=(tensor, matrix, tensor, matrix, matrix),
        check_vma=False,
    )
```
